512 devices in a mesh: replica: 16 (over y, core), fsdp: 32 (over x, z).
Axes of the slice: x: 4, y: 8, z: 8, core: 2. Of those that a mesh axis runs over, the one named last changes fastest.
Arguments:
- momentum: float32 [16, 256, 14336], P('replica', 'fsdp'), may hold values from -6 to 6
- gradient: bfloat16 [16, 256, 14336], P('replica', 'fsdp'), may hold values from -6 to 6
- selection: int32 [16, 4, 224, 2], replicated, may hold values from 0 to 63, as said below
Outputs:
- residual_momentum: float32 [16, 256, 14336], P('replica', 'fsdp')
- update: float32 [256, 14336], P(None, 'fsdp')
The draws below stay inside these ranges and needn't reach their ends.
Inputs may be any that keep to these rules, and one draw needn't show every extreme that they name: `selection`: for each replica and span, the 2 block numbers are distinct.
All inputs are finite; a program needn't handle non-finite values.
Results may differ from the reference program's by a relative error of at most 0.0003.
Values sent between devices are 32-bit elements; how exact they have to be, the bound alone decides.
A program may use at most 64 MiB of HBM per device.

```python
import jax
import jax.numpy as jnp
from jax import lax

COLUMNS = 14336
SPAN_SIDE = 64
BLOCK_SIDE = 8
BLOCKS_KEPT = 2
REPLICAS = 16
ROWS_ALL = 256
SPAN_ROWS = 4
SPAN_COLS = 224
BLOCKS = 64


def draw_selection(key, part):
    scores = jax.random.randint(key, (REPLICAS, SPAN_ROWS, SPAN_COLS, BLOCKS), 0, 1048576)
    scores = scores * BLOCKS + jnp.arange(BLOCKS, dtype=jnp.int32)
    order = jnp.argsort(scores, axis=-1)
    return order[..., :BLOCKS_KEPT].astype(jnp.int32)


def levels(rng, shape, cuts, least, largest):
    def one(axis_at, parts):
        draws = jax.random.uniform(jax.random.fold_in(jax.random.fold_in(rng, 6), axis_at), (parts,), jnp.float32, least / len(cuts), largest / len(cuts))
        return jnp.repeat(jnp.exp(draws), shape[axis_at] // parts).reshape((-1,) + (1,) * (len(shape) - axis_at - 1))

    level = one(*cuts[0])
    for cut in cuts[1:]:
        level = level * one(*cut)
    return level


def gaussian(stream_key, extent, scale, limit, pieces=(), held_as=jnp.bfloat16):
    level = levels(stream_key, extent, pieces, -0.22, 0.18) if pieces else 1.0
    array = jax.random.normal(stream_key, extent, jnp.float32) * scale * level
    return jnp.minimum(jnp.maximum(array, -limit), limit).astype(held_as)


def setup_inputs(seed: int = 0) -> dict:
    keys = jax.random.split(jax.random.key(seed), 4)
    return {
        "momentum": gaussian(keys[0], (REPLICAS, ROWS_ALL, COLUMNS), 1.0, 6.0, ((0, 16), (1, 32)), jnp.float32),
        "gradient": gaussian(keys[1], (REPLICAS, ROWS_ALL, COLUMNS), 1.0, 6.0, ((0, 16), (1, 32))),
        "selection": draw_selection(jax.random.fold_in(keys[3], 71), 0),
    }


decay_rate = 0.9
highest = lax.Precision.HIGHEST

def cosine_table(side):
    freq = jnp.arange(side, dtype=jnp.float32)[:, None]
    place = jnp.arange(side, dtype=jnp.float32)[None, :]
    scale = jnp.where(freq == 0, jnp.sqrt(1.0 / side), jnp.sqrt(2.0 / side))
    return scale * jnp.cos(jnp.pi * (2.0 * place + 1.0) * freq / (2.0 * side))

def block_mask(chosen):
    per_side = SPAN_SIDE // BLOCK_SIDE
    marks = (chosen[..., None] == jnp.arange(per_side * per_side, dtype=jnp.int32)).astype(jnp.float32)
    flags = lax.optimization_barrier(jnp.sum(marks, axis=-2))
    rows_c, cols_c = flags.shape[:2]
    grid = flags.reshape(rows_c, cols_c, per_side, 1, per_side, 1)
    grid = jnp.broadcast_to(grid, (rows_c, cols_c, per_side, BLOCK_SIDE, per_side, BLOCK_SIDE))
    return grid.reshape(rows_c, cols_c, SPAN_SIDE, SPAN_SIDE)

def reference(momentum, gradient, selection):
    table = cosine_table(SPAN_SIDE)

    def one_replica(total, items):
        moment, grad, chosen = items
        decayed = decay_rate * moment + grad.astype(jnp.float32)
        spans = decayed.reshape(SPAN_ROWS, SPAN_SIDE, SPAN_COLS, SPAN_SIDE)
        coeffs = jnp.einsum('ia,racb,jb->rcij', table, spans, table, precision=highest)
        kept = coeffs * block_mask(chosen)
        spatial = jnp.einsum('ia,rcij,jb->racb', table, kept, table, precision=highest)
        return (total + kept, decayed - spatial.reshape(ROWS_ALL, COLUMNS))
    start = jnp.zeros((SPAN_ROWS, SPAN_COLS, SPAN_SIDE, SPAN_SIDE), jnp.float32)
    total, residual_momentum = lax.scan(one_replica, start, (momentum, gradient, selection))
    update = jnp.einsum('ia,rcij,jb->racb', table, total, table, precision=highest)
    return (residual_momentum, update.reshape(ROWS_ALL, COLUMNS))
```

```python
import functools

import jax
import jax.numpy as jnp
import numpy as np
from jax import lax
from jax.experimental import pallas as pl
from jax.experimental.pallas import tpu as pltpu
from jax.sharding import PartitionSpec as P

SIDE = 64
BLOCK = 8
MESH = pl.DeviceIdType.MESH
F32 = jnp.float32
BF16 = jnp.bfloat16


def cosine_table():
    freq = np.arange(SIDE, dtype=np.float64)[:, None]
    place = np.arange(SIDE, dtype=np.float64)[None, :]
    scale = np.where(freq == 0, np.sqrt(1.0 / SIDE), np.sqrt(2.0 / SIDE))
    return scale * np.cos(np.pi * (2.0 * place + 1.0) * freq / (2.0 * SIDE))


def halves_np(value):
    value = value.astype(np.float32)
    high = value.astype(BF16)
    low = (value - high.astype(np.float32)).astype(BF16)
    return high, low


def tables(spans, devices_z):
    table = cosine_table()
    spread = np.zeros((8 * SIDE, 8, 8, BLOCK))
    for s in range(spans):
        spread[s * SIDE:(s + 1) * SIDE, :, s, :] = table.T.reshape(SIDE, 8, BLOCK)
    spread = np.stack(halves_np(spread.reshape(8 * SIDE, 8 * SIDE)))
    cube = table.reshape(8, BLOCK, devices_z, 8)
    by_a = cube.transpose(2, 3, 1, 0).reshape(devices_z, 64, 8)
    by_u = cube.transpose(2, 1, 3, 0).reshape(devices_z, 64, 8)
    rows = np.concatenate([by_a, by_u], axis=1)
    rows = np.concatenate(halves_np(rows), axis=-1)
    high, low = halves_np(table.T)
    inverse = np.concatenate([high, high, low], axis=1)
    return spread, rows, inverse


def halves(value):
    high = value.astype(BF16)
    low = (value - high.astype(F32)).astype(BF16)
    return high, low


def dot(a, b):
    return jnp.dot(a, b, preferred_element_type=F32)


def dot_t(a, b):
    return lax.dot_general(a, b, (((1,), (1,)), ((), ())), preferred_element_type=F32)


def kernel(
    nx, nz, nq, spans,
    mom_hbm, grad_hbm, sel_ref, spread_hbm, rows_hbm, inv_ref,
    res_ref, upd_ref,
    mom, grad, spread, rows, decayed, lhs, blk, blk_q, weights, part, arrived, kept, full, gathered, upd_half, res_buf,
    load_sem, send_sem, part_sem, full_sem, gather_sem, upd_send, upd_recv, out_sem,
):
    replica = lax.axis_index("replica")
    fsdp = lax.axis_index("fsdp")
    x, z = fsdp // nz, lax.rem(fsdp, nz)
    core = lax.rem(replica, 2)
    sibling = replica + 1 - 2 * core
    per_core = nx // 2
    width = spans * SIDE
    owners = nx * nz

    barrier = pltpu.get_barrier_semaphore()

    load_mom = pltpu.make_async_copy(mom_hbm, mom, load_sem.at[0])
    load_grad = pltpu.make_async_copy(grad_hbm, grad, load_sem.at[1])
    load_rows = pltpu.make_async_copy(rows_hbm.at[z], rows, load_sem.at[2])
    load_spread = pltpu.make_async_copy(spread_hbm, spread, load_sem.at[3])
    load_rows.start()
    load_mom.start()
    load_grad.start()
    load_spread.start()

    def greet_z(d, _):
        peer = x * nz + lax.rem(z + d, nz)
        pl.semaphore_signal(barrier, inc=1, device_id=(replica, peer), device_id_type=MESH)
        return 0

    lax.fori_loop(1, nz, greet_z, 0)

    def greet_plane(d, _):
        q = lax.rem(d, nq)
        xs = per_core * core + d // nq

        @pl.when(jnp.logical_or(q != replica, xs != x))
        def _():
            pl.semaphore_signal(barrier, inc=1, device_id=(q, xs * nz + z), device_id_type=MESH)

        return 0

    lax.fori_loop(0, per_core * nq, greet_plane, 0)
    pl.semaphore_signal(barrier, inc=1, device_id=(sibling, fsdp), device_id_type=MESH)

    lane = lax.broadcasted_iota(jnp.int32, (8, 128), 1)
    half = lane // 64
    sub16 = lax.broadcasted_iota(jnp.int32, (16, 128), 0) & 7

    all_cols = owners * spans
    at_own = (replica * nx + x) * 2
    col = lax.broadcasted_iota(jnp.int32, (owners, all_cols), 1)
    row = lax.broadcasted_iota(jnp.int32, (owners, all_cols), 0) * spans
    inside = jnp.logical_and(col >= row, col < row + spans)
    c_f = lax.broadcasted_iota(jnp.int32, (all_cols, 128), 0).astype(F32)
    c_mod = c_f - spans * jnp.floor((c_f + 0.5) * (1.0 / spans))
    l_i = lax.broadcasted_iota(jnp.int32, (all_cols, 128), 1)
    l_s = ((l_i & 63) // 8).astype(F32)
    placed = None
    for k in range(2):
        left = jnp.where(inside, jnp.broadcast_to(sel_ref[pl.ds(at_own + k, 1), :], (owners, all_cols)), 0).astype(F32)
        right = jnp.where(jnp.logical_and(c_mod == l_s, l_i // 64 == k), 1.0, 0.0)
        term = dot(left.astype(BF16), right.astype(BF16))
        placed = term if placed is None else placed + term
    blk[...] = placed.astype(jnp.int32)

    load_rows.wait()
    for f in range(0, owners, 2):
        ones = []
        for g in (f, f + 1):
            i_sel = jnp.broadcast_to(blk[g:g + 1, :], (16, 128)) // 8
            ones.append(jnp.where(i_sel == sub16, 1.0, 0.0).astype(BF16))
        weights[:, f * 128:(f + 2) * 128] = dot(rows[...], jnp.concatenate(ones, axis=1))

    load_mom.wait()
    load_grad.wait()
    decayed[...] = 0.9 * mom[...] + grad[...].astype(F32)

    for p in range(owners // 2):
        base = 2 * width * p
        even = decayed[:, base:base + 8 * SIDE]
        odd = pltpu.roll(decayed[:, base + width - 64:base + 2 * width], 8 * SIDE - 64, 1)
        high, low = halves(jnp.concatenate([even, odd], axis=0))
        lhs[0, 16 * p:16 * p + 16, :] = high
        lhs[1, 16 * p:16 * p + 16, :] = low

    load_spread.wait()

    def selected(f):
        both = jnp.broadcast_to(blk[f:f + 1, :], (8, 128)) & 7
        return both, pltpu.roll(both, 64, 1)

    group = 64
    for m in range(owners * 8 // group):
        at = slice(m * group, (m + 1) * group)
        coeff = dot(lhs[0, at, :], spread[0]) + dot(lhs[1, at, :], spread[0]) + dot(lhs[0, at, :], spread[1])
        for g in range(group // 8):
            f = m * (group // 8) + g
            j_own, j_other = selected(f)
            direct = other = jnp.zeros((8, 128), F32)
            for t in range(4):
                piece = coeff[8 * g:8 * g + 8, 128 * t:128 * t + 128]
                direct = jnp.where(j_own // 2 == t, piece, direct)
                other = jnp.where(j_other // 2 == t, piece, other)
            picked = jnp.where((j_own & 1) == half, direct, pltpu.roll(other, 64, 1))
            total = None
            for a in range(8):
                term = weights[8 * a:8 * a + 8, f * 128:f * 128 + 128] * jnp.broadcast_to(picked[a:a + 1, :], (8, 128))
                total = term if total is None else total + term
            part[f % nz, f // nz] = total

    pl.semaphore_wait(barrier, nz - 1 + per_core * 0 + nx * (nq // 2) - jnp.where(core == x // per_core, 1, 0) + 1)

    def send_part(d, _):
        zt = lax.rem(z + d, nz)
        pltpu.make_async_remote_copy(
            part.at[zt], arrived.at[z], send_sem.at[0], part_sem,
            device_id=(replica, x * nz + zt), device_id_type=MESH,
        ).start()
        return 0

    lax.fori_loop(1, nz, send_part, 0)
    local = pltpu.make_async_copy(part.at[z], arrived.at[z], part_sem)
    local.start()

    c_own = lax.broadcasted_iota(jnp.int32, (all_cols, 128), 0) - spans * fsdp
    s_own = (lax.broadcasted_iota(jnp.int32, (all_cols, 128), 1) & 63) // 8
    pick = jnp.where(jnp.logical_and(c_own == s_own, s_own < spans), 1.0, 0.0).astype(BF16)
    blk_q[...] = dot(sel_ref[...].astype(F32).astype(BF16), pick).astype(jnp.int32)

    pltpu.make_async_copy(arrived, arrived, part_sem).wait()
    for xt in range(nx):
        total = arrived[0, xt]
        for zs in range(1, nz):
            total = total + arrived[zs, xt]
        kept[xt] = total

    def send_plane(d, _):
        xt = d // (nq // 2)
        qt = 2 * lax.rem(d, nq // 2) + x // per_core

        slot = gathered.at[lax.rem(x, per_core) * nq + replica]

        @pl.when(jnp.logical_or(qt != replica, xt != x))
        def _():
            pltpu.make_async_remote_copy(
                kept.at[xt], slot, send_sem.at[1], gather_sem,
                device_id=(qt, xt * nz + z), device_id_type=MESH,
            ).start()

        @pl.when(jnp.logical_and(qt == replica, xt == x))
        def _():
            pltpu.make_async_copy(kept.at[xt], slot, gather_sem).start()

        return 0

    def send_full(d, _):
        zt = lax.rem(z + d, nz)
        pltpu.make_async_remote_copy(
            kept, full.at[z], send_sem.at[2], full_sem,
            device_id=(replica, x * nz + zt), device_id_type=MESH,
        ).start()
        return 0

    lax.fori_loop(1, nz, send_full, 0)
    lax.fori_loop(0, nx * (nq // 2), send_plane, 0)
    pltpu.make_async_copy(kept, full.at[z], full_sem).start()

    pltpu.make_async_copy(full, full, full_sem).wait()
    for p in range(owners // 2):
        parts = []
        for f in (2 * p, 2 * p + 1):
            j_own, j_other = selected(f)
            block = full[f % nz, f // nz]
            total = None
            for u in range(8):
                term = weights[64 + 8 * u:72 + 8 * u, f * 128:f * 128 + 128] * jnp.broadcast_to(block[u:u + 1, :], (8, 128))
                total = term if total is None else total + term
            other = pltpu.roll(total, 64, 1)
            parts.append(jnp.concatenate([
                jnp.where(j_own == 2 * t + half, total, 0.0) + jnp.where(j_other == 2 * t + half, other, 0.0)
                for t in range(4)
            ], axis=1))
        high, low = halves(jnp.concatenate(parts, axis=0))
        lhs[0, 16 * p:16 * p + 16, :] = high
        lhs[1, 16 * p:16 * p + 16, :] = low
    for m in range(owners * 8 // group):
        at = slice(m * group, (m + 1) * group)
        space = dot_t(lhs[0, at, :], spread[0]) + dot_t(lhs[1, at, :], spread[0]) + dot_t(lhs[0, at, :], spread[1])
        for g in range(0, group // 8, 2):
            f = m * (group // 8) + g
            pair = jnp.concatenate([space[8 * g:8 * g + 8, :width], space[8 * g + 8:8 * g + 16, :width]], axis=1)
            at_cols = slice(f * width, (f + 2) * width)
            res_buf[:, at_cols] = decayed[:, at_cols] - pair
    store_res = pltpu.make_async_copy(res_buf, res_ref, out_sem.at[0])
    store_res.start()

    pltpu.make_async_copy(gathered, gathered, gather_sem).wait()
    spatial = []
    for r in range(per_core):
        strips = []
        for t in range(4):
            def add_replica(q, sums, r=r, t=t):
                value = gathered[r * nq + q]
                at = (q * nx + per_core * core + r) * 2
                numbers = jnp.where(half == 0, jnp.broadcast_to(blk_q[pl.ds(at, 1), :], (8, 128)), jnp.broadcast_to(blk_q[pl.ds(at + 1, 1), :], (8, 128)))
                other_numbers = pltpu.roll(numbers, 64, 1)
                other = pltpu.roll(value, 64, 1)
                j_here = 2 * t + half
                here = jnp.where((numbers & 7) == j_here, value, 0.0)
                there = jnp.where((other_numbers & 7) == j_here, other, 0.0)
                i_here, i_there = numbers // 8, other_numbers // 8
                return tuple(
                    sums[i] + jnp.where(i_here == i, here, 0.0) + jnp.where(i_there == i, there, 0.0)
                    for i in range(8)
                )

            sums = lax.fori_loop(0, nq, add_replica, tuple(jnp.zeros((8, 128), F32) for _ in range(8)))
            strips.append(jnp.concatenate(sums, axis=0))
        high, low = halves(jnp.concatenate(strips, axis=1))
        spatial.append(dot(inv_ref[...], jnp.concatenate([high, low, high], axis=0)))
    high, low = halves(jnp.concatenate(spatial, axis=0))
    g_high, g_low = spread[0, :width, :], spread[1, :width, :]
    upd_half[...] = dot_t(g_high, high) + dot_t(g_high, low) + dot_t(g_low, high)
    lanes = per_core * SIDE
    place = upd_ref.at[:, pl.ds(pl.multiple_of(core * lanes, lanes), lanes)]
    send_upd = pltpu.make_async_remote_copy(
        upd_half, place, upd_send, upd_recv, device_id=(sibling, fsdp), device_id_type=MESH
    )
    send_upd.start()
    store_upd = pltpu.make_async_copy(upd_half, place, out_sem.at[1])
    store_upd.start()

    pltpu.make_async_copy(part.at[pl.ds(0, nz - 1)], part.at[pl.ds(0, nz - 1)], send_sem.at[0]).wait()
    pltpu.make_async_copy(full.at[pl.ds(0, nz - 1)], full.at[pl.ds(0, nz - 1)], send_sem.at[2]).wait()
    sent = gathered.at[pl.ds(1, per_core * nq - 1)]

    @pl.when(core == x // per_core)
    def _():
        pltpu.make_async_copy(sent, sent, send_sem.at[1]).wait()

    @pl.when(core != x // per_core)
    def _():
        pltpu.make_async_copy(gathered, gathered, send_sem.at[1]).wait()

    store_res.wait()
    store_upd.wait()
    send_upd.wait()


def local(nx, nz, nq, momentum, gradient, selection):
    rows_dev, all_width = momentum.shape[1:]
    owners = nx * nz
    width = all_width // owners
    spans = width // SIDE
    spread, rows, inverse = tables(spans, nz)
    sel = selection.transpose(0, 1, 3, 2).reshape(nq * nx * 2, owners * spans)
    per_core = nx // 2
    hbm = pl.BlockSpec(memory_space=pl.ANY)
    vmem = pl.BlockSpec(memory_space=pltpu.VMEM)
    dma = pltpu.SemaphoreType.DMA
    res, upd = pl.pallas_call(
        functools.partial(kernel, nx, nz, nq, spans),
        out_shape=(
            jax.ShapeDtypeStruct((rows_dev, all_width), F32),
            jax.ShapeDtypeStruct((width, nx * SIDE), F32),
        ),
        in_specs=[hbm, hbm, vmem, hbm, hbm, vmem],
        out_specs=(hbm, hbm),
        scratch_shapes=[
            pltpu.VMEM((rows_dev, all_width), F32),
            pltpu.VMEM((rows_dev, all_width), BF16),
            pltpu.VMEM(spread.shape, BF16),
            pltpu.VMEM(rows.shape[1:], BF16),
            pltpu.VMEM((rows_dev, all_width), F32),
            pltpu.VMEM((2, owners * 8, 8 * SIDE), BF16),
            pltpu.VMEM((owners, 128), jnp.int32),
            pltpu.VMEM((nq * nx * 2, 128), jnp.int32),
            pltpu.VMEM((128, owners * 128), F32),
            pltpu.VMEM((nz, nx, 8, 128), F32),
            pltpu.VMEM((nz, nx, 8, 128), F32),
            pltpu.VMEM((nx, 8, 128), F32),
            pltpu.VMEM((nz, nx, 8, 128), F32),
            pltpu.VMEM((per_core * nq, 8, 128), F32),
            pltpu.VMEM((width, per_core * SIDE), F32),
            pltpu.VMEM((rows_dev, all_width), F32),
            dma((4,)), dma((3,)), dma, dma, dma, dma, dma, dma((2,)),
        ],
        compiler_params=pltpu.CompilerParams(
            collective_id=0, has_side_effects=True, vmem_limit_bytes=24 * 1024 * 1024
        ),
    )(momentum[0], gradient[0], sel, jnp.asarray(spread), jnp.asarray(rows), jnp.asarray(inverse))
    return res[None], upd.T


def solution(mesh):
    nq = mesh.shape["replica"]
    nz = 8
    nx = mesh.shape["fsdp"] // nz
    return jax.shard_map(
        functools.partial(local, nx, nz, nq),
        mesh=mesh,
        in_specs=(P("replica", "fsdp", None), P("replica", "fsdp", None), P()),
        out_specs=(P("replica", "fsdp", None), P(None, "fsdp")),
        check_vma=False,
    )
```

```python
import functools

import jax
import jax.numpy as jnp
import numpy as np
from jax import lax
from jax.experimental import pallas as pl
from jax.experimental.pallas import tpu as pltpu
from jax.sharding import PartitionSpec as P

SIDE = 64
BLOCK = 8
MESH = pl.DeviceIdType.MESH
F32 = jnp.float32
BF16 = jnp.bfloat16


def cosine_table():
    freq = np.arange(SIDE, dtype=np.float64)[:, None]
    place = np.arange(SIDE, dtype=np.float64)[None, :]
    scale = np.where(freq == 0, np.sqrt(1.0 / SIDE), np.sqrt(2.0 / SIDE))
    return scale * np.cos(np.pi * (2.0 * place + 1.0) * freq / (2.0 * SIDE))


def halves_np(value):
    value = value.astype(np.float32)
    high = value.astype(BF16)
    low = (value - high.astype(np.float32)).astype(BF16)
    return high, low


def tables(spans, devices_z):
    table = cosine_table()
    spread = np.zeros((8 * SIDE, 8, 8, BLOCK))
    for s in range(spans):
        spread[s * SIDE:(s + 1) * SIDE, :, s, :] = table.T.reshape(SIDE, 8, BLOCK)
    spread = np.stack(halves_np(spread.reshape(8 * SIDE, 8 * SIDE)))
    cube = table.reshape(8, BLOCK, devices_z, 8)
    by_a = cube.transpose(2, 3, 1, 0).reshape(devices_z, 64, 8)
    by_u = cube.transpose(2, 1, 3, 0).reshape(devices_z, 64, 8)
    rows = np.concatenate([by_a, by_u], axis=1)
    rows = np.concatenate(halves_np(rows), axis=-1)
    high, low = halves_np(table.T)
    inverse = np.concatenate([high, high, low], axis=1)
    return spread, rows, inverse


def halves(value):
    high = value.astype(BF16)
    low = (value - high.astype(F32)).astype(BF16)
    return high, low


def dot(a, b):
    return jnp.dot(a, b, preferred_element_type=F32)


def dot_t(a, b):
    return lax.dot_general(a, b, (((1,), (1,)), ((), ())), preferred_element_type=F32)


def kernel(
    nx, nz, nq, spans,
    mom_hbm, grad_hbm, sel_hbm, spread_hbm, spread_t_hbm, rows_hbm, inv_hbm,
    res_ref, upd_ref,
    mom, grad, sel, sel_own, spread, spread_t, rows, inv, decayed, lhs, blk, blk_q, numbers, weights, weights_t,
    part, arrived, full, gathered, sums,
    load_sem, part_send, part_sem, full_send, full_sem, plane_send, plane_sem, upd_send, upd_sem,
):
    replica = lax.axis_index("replica")
    fsdp = lax.axis_index("fsdp")
    x, z = fsdp // nz, lax.rem(fsdp, nz)
    y, core = replica // 2, lax.rem(replica, 2)
    ny = nq // 2
    sibling = replica + 1 - 2 * core
    per_core = nx // 2
    core_to, row_to = x // per_core, lax.rem(x, per_core)
    keeps_own = core == core_to
    width = spans * SIDE
    owners = nx * nz
    all_cols = owners * spans

    def outward(n):
        return sorted(range(n), key=lambda d: -min(d, n - d))

    barrier = pltpu.get_barrier_semaphore()
    for dy in outward(ny):
        for c in range(2):
            q = 2 * lax.rem(y + dy, ny) + c
            for r in range(per_core):
                xs = per_core * core + r
                greet = functools.partial(
                    pl.semaphore_signal, barrier, inc=1, device_id=(q, xs * nz + z), device_id_type=MESH
                )
                if dy == 0:
                    pl.when(jnp.logical_or(q != replica, xs != x))(greet)
                else:
                    greet()
    for d in outward(nz)[:-1]:
        peer = x * nz + lax.rem(z + d, nz)
        pl.semaphore_signal(barrier, inc=1, device_id=(replica, peer), device_id_type=MESH)
    pl.semaphore_signal(barrier, inc=1, device_id=(sibling, fsdp), device_id_type=MESH)

    loads = [
        pltpu.make_async_copy(source, target, load_sem.at[n])
        for n, (source, target) in enumerate((
            (sel_hbm.at[replica, x], sel_own), (rows_hbm.at[z], rows), (mom_hbm, mom), (grad_hbm, grad),
            (spread_hbm, spread), (sel_hbm, sel), (spread_t_hbm, spread_t), (inv_hbm, inv),
        ))
    ]
    for load in loads:
        load.start()

    half = lax.broadcasted_iota(jnp.int32, (8, 128), 1) // 64
    sub16 = lax.broadcasted_iota(jnp.int32, (16, 128), 0) & 7

    col = lax.broadcasted_iota(jnp.int32, (owners, all_cols), 1)
    row = lax.broadcasted_iota(jnp.int32, (owners, all_cols), 0) * spans
    inside = jnp.logical_and(col >= row, col < row + spans)
    c_f = lax.broadcasted_iota(jnp.int32, (all_cols, 128), 0).astype(F32)
    c_mod = c_f - spans * jnp.floor((c_f + 0.5) * (1.0 / spans))
    l_i = lax.broadcasted_iota(jnp.int32, (all_cols, 128), 1)
    same_span = c_mod == ((l_i & 63) // 8).astype(F32)
    loads[0].wait()
    placed = None
    for k in range(2):
        left = jnp.where(inside, jnp.broadcast_to(sel_own[k:k + 1, :], (owners, all_cols)), 0).astype(F32)
        right = jnp.where(jnp.logical_and(same_span, l_i // 64 == k), 1.0, 0.0)
        term = dot(left.astype(BF16), right.astype(BF16))
        placed = term if placed is None else placed + term
    blk[...] = placed.astype(jnp.int32)

    def one_hot(f):
        ones = []
        for g in (f, f + 1):
            i_sel = jnp.broadcast_to(blk[g:g + 1, :], (16, 128)) // 8
            ones.append(jnp.where(i_sel == sub16, 1.0, 0.0).astype(BF16))
        return jnp.concatenate(ones, axis=1)

    loads[1].wait()
    for f in range(0, owners, 2):
        weights[:, f * 128:(f + 2) * 128] = dot(rows[:64, :], one_hot(f))

    loads[2].wait()
    loads[3].wait()
    decayed[...] = 0.9 * mom[...] + grad[...].astype(F32)

    def selected(f):
        both = jnp.broadcast_to(blk[f:f + 1, :], (8, 128)) & 7
        return both, pltpu.roll(both, 64, 1)

    def span_columns(zt, xt):
        base = (xt * nz + zt) // 2 * 2 * width
        if zt % 2 == 0:
            return decayed[:, base:base + 8 * SIDE]
        return pltpu.roll(decayed[:, base + width - SIDE:base + 2 * width], 8 * SIDE - SIDE, 1)

    def send_part(zt):
        pltpu.make_async_remote_copy(
            part.at[zt], arrived.at[lax.rem(z - zt + nz, nz) - 1], part_send, part_sem,
            device_id=(replica, x * nz + zt), device_id_type=MESH,
        ).start()

    tall = owners * 8 // 2
    for group in range(2):
        for zt in range(group * nz // 2, (group + 1) * nz // 2):
            for xt in range(0, nx, 2):
                at = zt * nx * 8 + xt * 8
                high, low = halves(jnp.concatenate([span_columns(zt, xt), span_columns(zt, xt + 1)], axis=0))
                lhs[0, at:at + 16, :] = high
                lhs[1, at:at + 16, :] = low
        if group == 0:
            loads[4].wait()
        at = slice(group * tall, (group + 1) * tall)
        coeff = dot(lhs[0, at, :], spread[0]) + dot(lhs[1, at, :], spread[0]) + dot(lhs[0, at, :], spread[1])
        for g in range(tall // 8):
            zt, xt = group * nz // 2 + g // nx, g % nx
            f = xt * nz + zt
            j_own, j_other = selected(f)
            direct = other = jnp.zeros((8, 128), F32)
            for t in range(4):
                piece = coeff[8 * g:8 * g + 8, 128 * t:128 * t + 128]
                direct = jnp.where(j_own // 2 == t, piece, direct)
                other = jnp.where(j_other // 2 == t, piece, other)
            picked = jnp.where((j_own & 1) == half, direct, pltpu.roll(other, 64, 1))
            total = None
            for a in range(8):
                term = weights[8 * a:8 * a + 8, f * 128:f * 128 + 128] * jnp.broadcast_to(picked[a:a + 1, :], (8, 128))
                total = term if total is None else total + term
            part[zt, xt] = total
        if group == 0:
            pl.semaphore_wait(barrier, nz - 1 + nx * ny - jnp.where(keeps_own, 1, 0) + 1)
        for zt in range(group * nz // 2, (group + 1) * nz // 2):
            pl.when(z != zt)(functools.partial(send_part, zt))

    for f in range(0, owners, 2):
        weights_t[:, f * 128:(f + 2) * 128] = dot(rows[64:, :], one_hot(f))
    loads[5].wait()
    c_own = lax.broadcasted_iota(jnp.int32, (all_cols, 128), 0) - spans * fsdp
    s_own = (lax.broadcasted_iota(jnp.int32, (all_cols, 128), 1) & 63) // 8
    pick = jnp.where(jnp.logical_and(c_own == s_own, s_own < spans), 1.0, 0.0).astype(BF16)
    blk_q[...] = dot(sel[...].reshape(nq * nx * 2, all_cols).astype(F32).astype(BF16), pick).astype(jnp.int32)

    around = sorted(range(ny), key=lambda d: (min(d, ny - d), d))
    tiles = [(d, c, r) for d in around for c in range(2) for r in range(per_core)]
    reach = [[n for n, (d, _, _) in enumerate(tiles) if min(d, ny - d) == g] for g in range(ny // 2 + 1)]
    row_half = half[:1]
    for n, (d, c, r) in enumerate(tiles):
        at = ((2 * lax.rem(y + d, ny) + c) * nx + per_core * core + r) * 2
        pair = jnp.where(row_half == 0, blk_q[pl.ds(at, 1), :], blk_q[pl.ds(at + 1, 1), :])
        numbers[0, n:n + 1, :] = pair
        numbers[1, n:n + 1, :] = pltpu.roll(pair, 64, 1)

    pltpu.make_async_copy(arrived, arrived, part_sem).wait()
    for xt in range(nx):
        total = part[z, xt]
        for d in range(nz - 1):
            total = total + arrived[d, xt]
        full[z, xt] = total

    for d in outward(nz)[:-1]:
        pltpu.make_async_remote_copy(
            full.at[z], full.at[z], full_send, full_sem,
            device_id=(replica, x * nz + lax.rem(z + d, nz)), device_id_type=MESH,
        ).start()

    def send_plane(dx, dy):
        xt = lax.rem(x + dx, nx)
        slot = around.index((ny - dy) % ny) * 2 * per_core + core * per_core + row_to
        pltpu.make_async_remote_copy(
            full.at[z, xt], gathered.at[slot], plane_send, plane_sem.at[min(dy, ny - dy)],
            device_id=(2 * lax.rem(y + dy, ny) + core_to, xt * nz + z), device_id_type=MESH,
        ).start()

    targets = [(dx, dy) for dx in range(nx) for dy in range(ny)]
    for dx, dy in sorted(targets, key=lambda t: -min(t[0], nx - t[0]) - min(t[1], ny - t[1])):
        send = functools.partial(send_plane, dx, dy)
        if dx == dy == 0:
            pl.when(jnp.logical_not(keeps_own))(send)
        else:
            send()

    @pl.when(keeps_own)
    def _():
        gathered[core * per_core + row_to] = full[z, x]

    def await_tiles(first, count, sem):
        ref = gathered.at[pl.ds(first, count)]
        pltpu.make_async_copy(ref, ref, sem).wait()

    def gather_group(g):
        slots = reach[g]
        if g == 0:
            pl.when(keeps_own)(lambda: await_tiles(1, len(slots) - 1, plane_sem.at[0]))
            pl.when(jnp.logical_not(keeps_own))(lambda: await_tiles(0, len(slots), plane_sem.at[0]))
        else:
            await_tiles(slots[0], len(slots), plane_sem.at[g])
        for r in range(per_core):
            mine = [n for n in slots if tiles[n][2] == r]
            values = [gathered[n] for n in mine]
            others = [pltpu.roll(value, 64, 1) for value in values]
            here = [jnp.broadcast_to(numbers[0, n:n + 1, :], (8, 128)) for n in mine]
            there = [jnp.broadcast_to(numbers[1, n:n + 1, :], (8, 128)) for n in mine]
            for t in range(4):
                j_t = 2 * t + half
                i_here = [jnp.where((b & 7) == j_t, b // 8, -1) for b in here]
                i_there = [jnp.where((b & 7) == j_t, b // 8, -1) for b in there]
                for i in range(8):
                    at = (slice(8 * i, 8 * i + 8), slice(128 * t, 128 * t + 128))
                    total = None if g == 0 else sums[r, at[0], at[1]]
                    for value, other, h, o in zip(values, others, i_here, i_there):
                        term = jnp.where(h == i, value, jnp.where(o == i, other, 0.0))
                        total = term if total is None else total + term
                    sums[r, at[0], at[1]] = total

    gather_group(0)
    gather_group(1)

    loads[6].wait()
    pltpu.make_async_copy(full.at[pl.ds(0, nz - 1)], full.at[pl.ds(0, nz - 1)], full_sem).wait()
    for p in range(owners // 2):
        parts = []
        for f in (2 * p, 2 * p + 1):
            j_own, j_other = selected(f)
            total = None
            for u in range(8):
                term = weights_t[8 * u:8 * u + 8, f * 128:f * 128 + 128] * jnp.broadcast_to(
                    full[f % nz, f // nz, u:u + 1, :], (8, 128)
                )
                total = term if total is None else total + term
            other = pltpu.roll(total, 64, 1)
            parts.append(jnp.concatenate([
                jnp.where(j_own == 2 * t + half, total, 0.0) + jnp.where(j_other == 2 * t + half, other, 0.0)
                for t in range(4)
            ], axis=1))
        high, low = halves(jnp.concatenate(parts, axis=0))
        lhs[0, 16 * p:16 * p + 16, :] = high
        lhs[1, 16 * p:16 * p + 16, :] = low
    for m in range(2):
        at = slice(m * tall, (m + 1) * tall)
        space = dot(lhs[0, at, :], spread_t[0]) + dot(lhs[1, at, :], spread_t[0]) + dot(lhs[0, at, :], spread_t[1])
        for g in range(0, tall // 8, 2):
            f = m * (tall // 8) + g
            pair = jnp.concatenate([space[8 * g:8 * g + 8, :width], space[8 * g + 8:8 * g + 16, :width]], axis=1)
            at_cols = slice(f * width, (f + 2) * width)
            res_ref[:, at_cols] = decayed[:, at_cols] - pair

    for g in range(2, len(reach)):
        gather_group(g)

    loads[7].wait()
    spatial = []
    for r in range(per_core):
        high, low = halves(sums[r])
        spatial.append(dot(inv[...], jnp.concatenate([high, low, high], axis=0)))
    high, low = halves(jnp.concatenate(spatial, axis=0))
    both = jnp.concatenate([high, low], axis=0)
    lanes = per_core * SIDE
    mine = pl.ds(pl.multiple_of(core * lanes, lanes), lanes)
    pieces = []
    tall = width // 2
    for m in range(2):
        at = slice(m * tall, (m + 1) * tall)
        wide = dot_t(spread[0, at, :], both)
        upd_ref[at, mine] = wide[:, :lanes] + wide[:, lanes:] + dot_t(spread[1, at, :], high)
        place = upd_ref.at[at, mine]
        piece = pltpu.make_async_remote_copy(
            place, place, upd_send.at[m], upd_sem.at[m], device_id=(sibling, fsdp), device_id_type=MESH
        )
        piece.start()
        pieces.append(piece)

    seven = full.at[pl.ds(0, nz - 1)]
    pltpu.make_async_copy(seven, seven, part_send).wait()
    pltpu.make_async_copy(seven, seven, full_send).wait()
    pl.when(keeps_own)(lambda: await_tiles(1, len(tiles) - 1, plane_send))
    pl.when(jnp.logical_not(keeps_own))(lambda: await_tiles(0, len(tiles), plane_send))
    for piece in pieces:
        piece.wait()


def local(nx, nz, nq, momentum, gradient, selection):
    rows_dev, all_width = momentum.shape[1:]
    owners = nx * nz
    width = all_width // owners
    spans = width // SIDE
    spread, rows, inverse = tables(spans, nz)
    sel = selection.transpose(0, 1, 3, 2)
    spread_t = spread.transpose(0, 2, 1)
    per_core = nx // 2
    hbm = pl.BlockSpec(memory_space=pltpu.HBM)
    vmem = pl.BlockSpec(memory_space=pltpu.VMEM)
    dma = pltpu.SemaphoreType.DMA
    slab = (rows_dev, all_width)
    res, upd = pl.pallas_call(
        functools.partial(kernel, nx, nz, nq, spans),
        out_shape=(
            jax.ShapeDtypeStruct(slab, F32),
            jax.ShapeDtypeStruct((width, nx * SIDE), F32),
        ),
        in_specs=[hbm] * 7,
        out_specs=(vmem, vmem),
        scratch_shapes=[
            pltpu.VMEM(slab, F32),
            pltpu.VMEM(slab, BF16),
            pltpu.VMEM(sel.shape, jnp.int32),
            pltpu.VMEM(sel.shape[2:], jnp.int32),
            pltpu.VMEM(spread.shape, BF16),
            pltpu.VMEM(spread.shape, BF16),
            pltpu.VMEM(rows.shape[1:], BF16),
            pltpu.VMEM(inverse.shape, BF16),
            pltpu.VMEM(slab, F32),
            pltpu.VMEM((2, owners * 8, 8 * SIDE), BF16),
            pltpu.VMEM((owners, 128), jnp.int32),
            pltpu.VMEM((nq * nx * 2, 128), jnp.int32),
            pltpu.VMEM((2, nq * per_core, 128), jnp.int32),
            pltpu.VMEM((64, owners * 128), F32),
            pltpu.VMEM((64, owners * 128), F32),
            pltpu.VMEM((nz, nx, 8, 128), F32),
            pltpu.VMEM((nz - 1, nx, 8, 128), F32),
            pltpu.VMEM((nz, nx, 8, 128), F32),
            pltpu.VMEM((nq * per_core, 8, 128), F32),
            pltpu.VMEM((per_core, SIDE, 8 * SIDE), F32),
            dma((8,)), dma, dma, dma, dma, dma, dma((nq // 4 + 1,)), dma((2,)), dma((2,)),
        ],
        compiler_params=pltpu.CompilerParams(
            collective_id=0, has_side_effects=True, vmem_limit_bytes=62 * 1024 * 1024
        ),
    )(momentum[0], gradient[0], sel, jnp.asarray(spread), jnp.asarray(spread_t), jnp.asarray(rows), jnp.asarray(inverse))
    return res[None], upd.T


def solution(mesh):
    nq = mesh.shape["replica"]
    nz = 8
    nx = mesh.shape["fsdp"] // nz
    return jax.shard_map(
        functools.partial(local, nx, nz, nq),
        mesh=mesh,
        in_specs=(P("replica", "fsdp", None), P("replica", "fsdp", None), P()),
        out_specs=(P("replica", "fsdp", None), P(None, "fsdp")),
        check_vma=False,
    )
```

```python
import functools

import jax
import jax.numpy as jnp
import numpy as np
from jax import lax
from jax.experimental import pallas as pl
from jax.experimental.pallas import tpu as pltpu
from jax.sharding import PartitionSpec as P

SIDE = 64
BLOCK = 8
MESH = pl.DeviceIdType.MESH
F32 = jnp.float32
BF16 = jnp.bfloat16


def cosine_table():
    freq = np.arange(SIDE, dtype=np.float64)[:, None]
    place = np.arange(SIDE, dtype=np.float64)[None, :]
    scale = np.where(freq == 0, np.sqrt(1.0 / SIDE), np.sqrt(2.0 / SIDE))
    return scale * np.cos(np.pi * (2.0 * place + 1.0) * freq / (2.0 * SIDE))


def halves_np(value):
    value = value.astype(np.float32)
    high = value.astype(BF16)
    low = (value - high.astype(np.float32)).astype(BF16)
    return high, low


def tables(spans, devices_z):
    table = cosine_table()
    spread = np.zeros((8 * SIDE, 8, 8, BLOCK))
    for s in range(spans):
        spread[s * SIDE:(s + 1) * SIDE, :, s, :] = table.T.reshape(SIDE, 8, BLOCK)
    spread = np.stack(halves_np(spread.reshape(8 * SIDE, 8 * SIDE)))
    cube = table.reshape(8, BLOCK, devices_z, 8)
    by_a = cube.transpose(2, 3, 1, 0).reshape(devices_z, 64, 8)
    by_u = cube.transpose(2, 1, 3, 0).reshape(devices_z, 64, 8)
    rows = np.concatenate([by_a, by_u], axis=1)
    rows = np.concatenate(halves_np(rows), axis=-1)
    high, low = halves_np(table.T)
    inverse = np.concatenate([high, high, low], axis=1)
    return spread, rows, inverse


def halves(value):
    high = value.astype(BF16)
    low = (value - high.astype(F32)).astype(BF16)
    return high, low


def dot(a, b):
    return jnp.dot(a, b, preferred_element_type=F32)


def dot_t(a, b):
    return lax.dot_general(a, b, (((1,), (1,)), ((), ())), preferred_element_type=F32)


def kernel(
    nx, nz, nq, spans,
    mom_hbm, grad_hbm, sel_hbm, spread_hbm, spread_t_hbm, rows_hbm, inv_hbm,
    res_ref, upd_ref,
    mom, grad, sel, sel_own, spread, spread_t, rows, inv, decayed, lhs, blk, blk_q, numbers, weights, weights_t,
    part, arrived, full, gathered, sums,
    load_sem, part_send, part_sem, full_send, full_sem, plane_send, plane_sem, upd_send, upd_sem,
):
    replica = lax.axis_index("replica")
    fsdp = lax.axis_index("fsdp")
    x, z = fsdp // nz, lax.rem(fsdp, nz)
    y, core = replica // 2, lax.rem(replica, 2)
    ny = nq // 2
    sibling = replica + 1 - 2 * core
    per_core = nx // 2
    core_to, row_to = x // per_core, lax.rem(x, per_core)
    keeps_own = core == core_to
    width = spans * SIDE
    owners = nx * nz
    all_cols = owners * spans

    def outward(n):
        return sorted(range(n), key=lambda d: -min(d, n - d))

    barrier = pltpu.get_barrier_semaphore()
    for d in outward(nz)[:-1]:
        peer = x * nz + lax.rem(z + d, nz)
        pl.semaphore_signal(barrier, inc=1, device_id=(replica, peer), device_id_type=MESH)
    for dy in outward(ny):
        for c in range(2):
            q = 2 * lax.rem(y + dy, ny) + c
            for r in range(per_core):
                xs = per_core * core + r
                greet = functools.partial(
                    pl.semaphore_signal, barrier, inc=1, device_id=(q, xs * nz + z), device_id_type=MESH
                )
                if dy == 0:
                    pl.when(jnp.logical_or(q != replica, xs != x))(greet)
                else:
                    greet()
    pl.semaphore_signal(barrier, inc=1, device_id=(sibling, fsdp), device_id_type=MESH)

    loads = [
        pltpu.make_async_copy(source, target, load_sem.at[n])
        for n, (source, target) in enumerate((
            (sel_hbm.at[replica, x], sel_own), (rows_hbm.at[z], rows), (mom_hbm, mom), (grad_hbm, grad),
            (spread_hbm, spread), (sel_hbm, sel), (spread_t_hbm, spread_t), (inv_hbm, inv),
        ))
    ]
    for load in loads[:5]:
        load.start()

    half = lax.broadcasted_iota(jnp.int32, (8, 128), 1) // 64
    sub16 = lax.broadcasted_iota(jnp.int32, (16, 128), 0) & 7

    col = lax.broadcasted_iota(jnp.int32, (owners, all_cols), 1)
    row = lax.broadcasted_iota(jnp.int32, (owners, all_cols), 0) * spans
    inside = jnp.logical_and(col >= row, col < row + spans)
    c_f = lax.broadcasted_iota(jnp.int32, (all_cols, 128), 0).astype(F32)
    c_mod = c_f - spans * jnp.floor((c_f + 0.5) * (1.0 / spans))
    l_i = lax.broadcasted_iota(jnp.int32, (all_cols, 128), 1)
    same_span = c_mod == ((l_i & 63) // 8).astype(F32)
    loads[0].wait()
    placed = None
    for k in range(2):
        left = jnp.where(inside, jnp.broadcast_to(sel_own[k:k + 1, :], (owners, all_cols)), 0).astype(F32)
        right = jnp.where(jnp.logical_and(same_span, l_i // 64 == k), 1.0, 0.0)
        term = dot(left.astype(BF16), right.astype(BF16))
        placed = term if placed is None else placed + term
    blk[...] = placed.astype(jnp.int32)

    def one_hot(f):
        ones = []
        for g in (f, f + 1):
            i_sel = jnp.broadcast_to(blk[g:g + 1, :], (16, 128)) // 8
            ones.append(jnp.where(i_sel == sub16, 1.0, 0.0).astype(BF16))
        return jnp.concatenate(ones, axis=1)

    loads[1].wait()
    for f in range(0, owners, 2):
        weights[:, f * 128:(f + 2) * 128] = dot(rows[:64, :], one_hot(f))

    loads[2].wait()
    loads[3].wait()
    decayed[...] = 0.9 * mom[...] + grad[...].astype(F32)

    def selected(f):
        both = jnp.broadcast_to(blk[f:f + 1, :], (8, 128)) & 7
        return both, pltpu.roll(both, 64, 1)

    def span_columns(zt, xt):
        base = (xt * nz + zt) // 2 * 2 * width
        if zt % 2 == 0:
            return decayed[:, base:base + 8 * SIDE]
        return pltpu.roll(decayed[:, base + width - SIDE:base + 2 * width], 8 * SIDE - SIDE, 1)

    def send_part(zt):
        pltpu.make_async_remote_copy(
            part.at[zt], arrived.at[lax.rem(z - zt + nz, nz) - 1], part_send, part_sem,
            device_id=(replica, x * nz + zt), device_id_type=MESH,
        ).start()

    tall = owners * 8 // 2
    for group in range(2):
        for zt in range(group * nz // 2, (group + 1) * nz // 2):
            for xt in range(0, nx, 2):
                at = zt * nx * 8 + xt * 8
                high, low = halves(jnp.concatenate([span_columns(zt, xt), span_columns(zt, xt + 1)], axis=0))
                lhs[0, at:at + 16, :] = high
                lhs[1, at:at + 16, :] = low
        if group == 0:
            loads[4].wait()
        at = slice(group * tall, (group + 1) * tall)
        coeff = dot(lhs[0, at, :], spread[0]) + dot(lhs[1, at, :], spread[0]) + dot(lhs[0, at, :], spread[1])
        for g in range(tall // 8):
            zt, xt = group * nz // 2 + g // nx, g % nx
            f = xt * nz + zt
            j_own, j_other = selected(f)
            direct = other = jnp.zeros((8, 128), F32)
            for t in range(4):
                piece = coeff[8 * g:8 * g + 8, 128 * t:128 * t + 128]
                direct = jnp.where(j_own // 2 == t, piece, direct)
                other = jnp.where(j_other // 2 == t, piece, other)
            picked = jnp.where((j_own & 1) == half, direct, pltpu.roll(other, 64, 1))
            total = None
            for a in range(8):
                term = weights[8 * a:8 * a + 8, f * 128:f * 128 + 128] * jnp.broadcast_to(picked[a:a + 1, :], (8, 128))
                total = term if total is None else total + term
            part[zt, xt] = total
        if group == 0:
            pl.semaphore_wait(barrier, nz - 1 + nx * ny - jnp.where(keeps_own, 1, 0) + 1)
        for zt in range(group * nz // 2, (group + 1) * nz // 2):
            pl.when(z != zt)(functools.partial(send_part, zt))

    for load in loads[5:]:
        load.start()

    for f in range(0, owners, 2):
        weights_t[:, f * 128:(f + 2) * 128] = dot(rows[64:, :], one_hot(f))
    loads[5].wait()
    c_own = lax.broadcasted_iota(jnp.int32, (all_cols, 128), 0) - spans * fsdp
    s_own = (lax.broadcasted_iota(jnp.int32, (all_cols, 128), 1) & 63) // 8
    pick = jnp.where(jnp.logical_and(c_own == s_own, s_own < spans), 1.0, 0.0).astype(BF16)
    blk_q[...] = dot(sel[...].reshape(nq * nx * 2, all_cols).astype(F32).astype(BF16), pick).astype(jnp.int32)

    around = sorted(range(ny), key=lambda d: (min(d, ny - d), d))
    tiles = [(d, c, r) for d in around for c in range(2) for r in range(per_core)]
    reach = [[n for n, (d, _, _) in enumerate(tiles) if min(d, ny - d) == g] for g in range(ny // 2 + 1)]
    row_half = half[:1]
    for n, (d, c, r) in enumerate(tiles):
        at = ((2 * lax.rem(y + d, ny) + c) * nx + per_core * core + r) * 2
        pair = jnp.where(row_half == 0, blk_q[pl.ds(at, 1), :], blk_q[pl.ds(at + 1, 1), :])
        numbers[0, n:n + 1, :] = pair
        numbers[1, n:n + 1, :] = pltpu.roll(pair, 64, 1)

    pltpu.make_async_copy(arrived, arrived, part_sem).wait()
    for xt in range(nx):
        total = part[z, xt]
        for d in range(nz - 1):
            total = total + arrived[d, xt]
        full[z, xt] = total

    for d in outward(nz)[:-1]:
        pltpu.make_async_remote_copy(
            full.at[z], full.at[z], full_send, full_sem,
            device_id=(replica, x * nz + lax.rem(z + d, nz)), device_id_type=MESH,
        ).start()

    def send_plane(dx, dy):
        xt = lax.rem(x + dx, nx)
        slot = around.index((ny - dy) % ny) * 2 * per_core + core * per_core + row_to
        pltpu.make_async_remote_copy(
            full.at[z, xt], gathered.at[slot], plane_send, plane_sem.at[min(dy, ny - dy)],
            device_id=(2 * lax.rem(y + dy, ny) + core_to, xt * nz + z), device_id_type=MESH,
        ).start()

    targets = [(dx, dy) for dx in range(nx) for dy in range(ny)]
    for dx, dy in sorted(targets, key=lambda t: -min(t[0], nx - t[0]) - min(t[1], ny - t[1])):
        send = functools.partial(send_plane, dx, dy)
        if dx == dy == 0:
            pl.when(jnp.logical_not(keeps_own))(send)
        else:
            send()

    @pl.when(keeps_own)
    def _():
        gathered[core * per_core + row_to] = full[z, x]

    def await_tiles(first, count, sem):
        ref = gathered.at[pl.ds(first, count)]
        pltpu.make_async_copy(ref, ref, sem).wait()

    def gather_group(g):
        slots = reach[g]
        if g == 0:
            pl.when(keeps_own)(lambda: await_tiles(1, len(slots) - 1, plane_sem.at[0]))
            pl.when(jnp.logical_not(keeps_own))(lambda: await_tiles(0, len(slots), plane_sem.at[0]))
        else:
            await_tiles(slots[0], len(slots), plane_sem.at[g])
        for r in range(per_core):
            mine = [n for n in slots if tiles[n][2] == r]
            values = [gathered[n] for n in mine]
            others = [pltpu.roll(value, 64, 1) for value in values]
            here = [jnp.broadcast_to(numbers[0, n:n + 1, :], (8, 128)) for n in mine]
            there = [jnp.broadcast_to(numbers[1, n:n + 1, :], (8, 128)) for n in mine]
            for t in range(4):
                j_t = 2 * t + half
                i_here = [jnp.where((b & 7) == j_t, b // 8, -1) for b in here]
                i_there = [jnp.where((b & 7) == j_t, b // 8, -1) for b in there]
                for i in range(8):
                    at = (slice(8 * i, 8 * i + 8), slice(128 * t, 128 * t + 128))
                    total = None if g == 0 else sums[r, at[0], at[1]]
                    for value, other, h, o in zip(values, others, i_here, i_there):
                        term = jnp.where(h == i, value, jnp.where(o == i, other, 0.0))
                        total = term if total is None else total + term
                    sums[r, at[0], at[1]] = total

    gather_group(0)
    gather_group(1)

    loads[6].wait()
    pltpu.make_async_copy(full.at[pl.ds(0, nz - 1)], full.at[pl.ds(0, nz - 1)], full_sem).wait()
    for p in range(owners // 2):
        parts = []
        for f in (2 * p, 2 * p + 1):
            j_own, j_other = selected(f)
            total = None
            for u in range(8):
                term = weights_t[8 * u:8 * u + 8, f * 128:f * 128 + 128] * jnp.broadcast_to(
                    full[f % nz, f // nz, u:u + 1, :], (8, 128)
                )
                total = term if total is None else total + term
            other = pltpu.roll(total, 64, 1)
            parts.append(jnp.concatenate([
                jnp.where(j_own == 2 * t + half, total, 0.0) + jnp.where(j_other == 2 * t + half, other, 0.0)
                for t in range(4)
            ], axis=1))
        high, low = halves(jnp.concatenate(parts, axis=0))
        lhs[0, 16 * p:16 * p + 16, :] = high
        lhs[1, 16 * p:16 * p + 16, :] = low
    for m in range(2):
        at = slice(m * tall, (m + 1) * tall)
        space = dot(lhs[0, at, :], spread_t[0]) + dot(lhs[1, at, :], spread_t[0]) + dot(lhs[0, at, :], spread_t[1])
        for g in range(0, tall // 8, 2):
            f = m * (tall // 8) + g
            pair = jnp.concatenate([space[8 * g:8 * g + 8, :width], space[8 * g + 8:8 * g + 16, :width]], axis=1)
            at_cols = slice(f * width, (f + 2) * width)
            res_ref[:, at_cols] = decayed[:, at_cols] - pair

    for g in range(2, len(reach)):
        gather_group(g)

    loads[7].wait()
    spatial = []
    for r in range(per_core):
        high, low = halves(sums[r])
        spatial.append(dot(inv[...], jnp.concatenate([high, low, high], axis=0)))
    high, low = halves(jnp.concatenate(spatial, axis=0))
    both = jnp.concatenate([high, low], axis=0)
    lanes = per_core * SIDE
    mine = pl.ds(pl.multiple_of(core * lanes, lanes), lanes)
    pieces = []
    tall = width // 2
    for m in range(2):
        at = slice(m * tall, (m + 1) * tall)
        wide = dot_t(spread[0, at, :], both)
        upd_ref[at, mine] = wide[:, :lanes] + wide[:, lanes:] + dot_t(spread[1, at, :], high)
        place = upd_ref.at[at, mine]
        piece = pltpu.make_async_remote_copy(
            place, place, upd_send.at[m], upd_sem.at[m], device_id=(sibling, fsdp), device_id_type=MESH
        )
        piece.start()
        pieces.append(piece)

    seven = full.at[pl.ds(0, nz - 1)]
    pltpu.make_async_copy(seven, seven, part_send).wait()
    pltpu.make_async_copy(seven, seven, full_send).wait()
    pl.when(keeps_own)(lambda: await_tiles(1, len(tiles) - 1, plane_send))
    pl.when(jnp.logical_not(keeps_own))(lambda: await_tiles(0, len(tiles), plane_send))
    for piece in pieces:
        piece.wait()


def store_kernel(res_vmem, upd_vmem, res_ref, upd_ref, sems):
    stores = [
        pltpu.make_async_copy(source, target, sems.at[n])
        for n, (source, target) in enumerate(((res_vmem, res_ref), (upd_vmem, upd_ref)))
    ]
    for store in stores:
        store.start()
    for store in stores:
        store.wait()


def local(nx, nz, nq, momentum, gradient, selection):
    rows_dev, all_width = momentum.shape[1:]
    owners = nx * nz
    width = all_width // owners
    spans = width // SIDE
    spread, rows, inverse = tables(spans, nz)
    sel = selection.transpose(0, 1, 3, 2)
    spread_t = spread.transpose(0, 2, 1)
    per_core = nx // 2
    hbm = pl.BlockSpec(memory_space=pltpu.HBM)
    vmem = pl.BlockSpec(memory_space=pltpu.VMEM)
    dma = pltpu.SemaphoreType.DMA
    slab = (rows_dev, all_width)
    operands = (momentum[0], gradient[0], sel, *map(jnp.asarray, (spread, spread_t, rows, inverse)))
    res, upd = pl.pallas_call(
        functools.partial(kernel, nx, nz, nq, spans),
        out_shape=(
            pltpu.VMEM(slab, F32),
            pltpu.VMEM((width, nx * SIDE), F32),
        ),
        in_specs=[hbm] * 7,
        out_specs=(vmem, vmem),
        scratch_shapes=[
            pltpu.VMEM(slab, F32),
            pltpu.VMEM(slab, BF16),
            pltpu.VMEM(sel.shape, jnp.int32),
            pltpu.VMEM(sel.shape[2:], jnp.int32),
            pltpu.VMEM(spread.shape, BF16),
            pltpu.VMEM(spread.shape, BF16),
            pltpu.VMEM(rows.shape[1:], BF16),
            pltpu.VMEM(inverse.shape, BF16),
            pltpu.VMEM(slab, F32),
            pltpu.VMEM((2, owners * 8, 8 * SIDE), BF16),
            pltpu.VMEM((owners, 128), jnp.int32),
            pltpu.VMEM((nq * nx * 2, 128), jnp.int32),
            pltpu.VMEM((2, nq * per_core, 128), jnp.int32),
            pltpu.VMEM((64, owners * 128), F32),
            pltpu.VMEM((64, owners * 128), F32),
            pltpu.VMEM((nz, nx, 8, 128), F32),
            pltpu.VMEM((nz - 1, nx, 8, 128), F32),
            pltpu.VMEM((nz, nx, 8, 128), F32),
            pltpu.VMEM((nq * per_core, 8, 128), F32),
            pltpu.VMEM((per_core, SIDE, 8 * SIDE), F32),
            dma((8,)), dma, dma, dma, dma, dma, dma((nq // 4 + 1,)), dma((2,)), dma((2,)),
        ],
        compiler_params=pltpu.CompilerParams(
            collective_id=0, has_side_effects=True, vmem_limit_bytes=24 * 1024 * 1024
        ),
    )(*(pltpu.with_memory_space_constraint(array, pltpu.HBM) for array in operands))
    res, upd = pl.pallas_call(
        store_kernel,
        out_shape=(jax.ShapeDtypeStruct(slab, F32), jax.ShapeDtypeStruct(upd.shape, F32)),
        in_specs=[vmem] * 2,
        out_specs=(hbm, hbm),
        scratch_shapes=[dma((2,))],
        compiler_params=pltpu.CompilerParams(vmem_limit_bytes=4 * 1024 * 1024),
    )(*(pltpu.with_memory_space_constraint(array, pltpu.VMEM) for array in (res, upd)))
    return res[None], upd.T


def solution(mesh):
    nq = mesh.shape["replica"]
    nz = 8
    nx = mesh.shape["fsdp"] // nz
    return jax.shard_map(
        functools.partial(local, nx, nz, nq),
        mesh=mesh,
        in_specs=(P("replica", "fsdp", None), P("replica", "fsdp", None), P()),
        out_specs=(P("replica", "fsdp", None), P(None, "fsdp")),
        check_vma=False,
    )
```

```python
import functools

import jax
import jax.numpy as jnp
import numpy as np
from jax import lax
from jax.experimental import pallas as pl
from jax.experimental.pallas import tpu as pltpu
from jax.sharding import PartitionSpec as P

SIDE = 64
BLOCK = 8
MESH = pl.DeviceIdType.MESH
F32 = jnp.float32
BF16 = jnp.bfloat16


def cosine_table():
    freq = np.arange(SIDE, dtype=np.float64)[:, None]
    place = np.arange(SIDE, dtype=np.float64)[None, :]
    scale = np.where(freq == 0, np.sqrt(1.0 / SIDE), np.sqrt(2.0 / SIDE))
    return scale * np.cos(np.pi * (2.0 * place + 1.0) * freq / (2.0 * SIDE))


def halves_np(value):
    value = value.astype(np.float32)
    high = value.astype(BF16)
    low = (value - high.astype(np.float32)).astype(BF16)
    return high, low


def tables(spans, devices_z):
    table = cosine_table()
    spread = np.zeros((8 * SIDE, 8, 8, BLOCK))
    for s in range(spans):
        spread[s * SIDE:(s + 1) * SIDE, :, s, :] = table.T.reshape(SIDE, 8, BLOCK)
    spread = np.stack(halves_np(spread.reshape(8 * SIDE, 8 * SIDE)))
    cube = table.reshape(8, BLOCK, devices_z, 8)
    by_a = cube.transpose(2, 3, 1, 0).reshape(devices_z, 64, 8)
    by_u = cube.transpose(2, 1, 3, 0).reshape(devices_z, 64, 8)
    rows = np.concatenate([by_a, by_u], axis=1)
    rows = np.concatenate(halves_np(rows), axis=-1)
    high, low = halves_np(np.kron(np.eye(2), table))
    inverse = np.concatenate([high, high, low], axis=0)
    return spread, rows, inverse


def halves(value):
    high = value.astype(BF16)
    low = (value - high.astype(F32)).astype(BF16)
    return high, low


def dot(a, b):
    return jnp.dot(a, b, preferred_element_type=F32)


def kernel(
    nx, nz, nq, spans,
    mom_hbm, grad_hbm, sel_hbm, spread_hbm, spread_t_hbm, rows_hbm, inv_hbm,
    res_ref, upd_ref,
    mom, grad, sel, sel_own, spread, spread_t, rows, inv, decayed, lhs, blk, blk_q, numbers, weights, weights_t,
    part, arrived, full, gathered, sums,
    load_sem, part_send, part_sem, full_send, full_sem, plane_send, plane_sem, upd_send, upd_sem,
):
    replica = lax.axis_index("replica")
    fsdp = lax.axis_index("fsdp")
    x, z = fsdp // nz, lax.rem(fsdp, nz)
    y, core = replica // 2, lax.rem(replica, 2)
    ny = nq // 2
    sibling = replica + 1 - 2 * core
    per_core = nx // 2
    core_to, row_to = x // per_core, lax.rem(x, per_core)
    keeps_own = core == core_to
    width = spans * SIDE
    owners = nx * nz
    all_cols = owners * spans

    def outward(n):
        return sorted(range(n), key=lambda d: -min(d, n - d))

    barrier = pltpu.get_barrier_semaphore()
    for d in outward(nz)[:-1]:
        peer = x * nz + lax.rem(z + d, nz)
        pl.semaphore_signal(barrier, inc=1, device_id=(replica, peer), device_id_type=MESH)
    for dy in outward(ny):
        for c in range(2):
            q = 2 * lax.rem(y + dy, ny) + c
            for r in range(per_core):
                xs = per_core * core + r
                greet = functools.partial(
                    pl.semaphore_signal, barrier, inc=1, device_id=(q, xs * nz + z), device_id_type=MESH
                )
                if dy == 0:
                    pl.when(jnp.logical_or(q != replica, xs != x))(greet)
                else:
                    greet()
    pl.semaphore_signal(barrier, inc=1, device_id=(sibling, fsdp), device_id_type=MESH)

    loads = [
        pltpu.make_async_copy(source, target, load_sem.at[n])
        for n, (source, target) in enumerate((
            (sel_hbm.at[replica, x], sel_own), (rows_hbm.at[z], rows), (mom_hbm, mom), (grad_hbm, grad),
            (spread_hbm, spread), (sel_hbm, sel), (spread_t_hbm, spread_t), (inv_hbm, inv),
        ))
    ]
    for load in loads[:5]:
        load.start()

    half = lax.broadcasted_iota(jnp.int32, (8, 128), 1) // 64
    sub16 = lax.broadcasted_iota(jnp.int32, (16, 128), 0) & 7

    col = lax.broadcasted_iota(jnp.int32, (owners, all_cols), 1)
    row = lax.broadcasted_iota(jnp.int32, (owners, all_cols), 0) * spans
    inside = jnp.logical_and(col >= row, col < row + spans)
    c_f = lax.broadcasted_iota(jnp.int32, (all_cols, 128), 0).astype(F32)
    c_mod = c_f - spans * jnp.floor((c_f + 0.5) * (1.0 / spans))
    l_i = lax.broadcasted_iota(jnp.int32, (all_cols, 128), 1)
    same_span = c_mod == ((l_i & 63) // 8).astype(F32)
    loads[0].wait()
    placed = None
    for k in range(2):
        left = jnp.where(inside, jnp.broadcast_to(sel_own[k:k + 1, :], (owners, all_cols)), 0).astype(F32)
        right = jnp.where(jnp.logical_and(same_span, l_i // 64 == k), 1.0, 0.0)
        term = dot(left.astype(BF16), right.astype(BF16))
        placed = term if placed is None else placed + term
    blk[...] = placed.astype(jnp.int32)

    def one_hot(f):
        ones = []
        for g in (f, f + 1):
            i_sel = jnp.broadcast_to(blk[g:g + 1, :], (16, 128)) // 8
            ones.append(jnp.where(i_sel == sub16, 1.0, 0.0).astype(BF16))
        return jnp.concatenate(ones, axis=1)

    loads[1].wait()
    for f in range(0, owners, 2):
        weights[:, f * 128:(f + 2) * 128] = dot(rows[:64, :], one_hot(f))

    loads[2].wait()
    loads[3].wait()
    decayed[...] = 0.9 * mom[...] + grad[...].astype(F32)

    def selected(f):
        both = jnp.broadcast_to(blk[f:f + 1, :], (8, 128)) & 7
        return both, pltpu.roll(both, 64, 1)

    def span_columns(zt, xt):
        base = (xt * nz + zt) // 2 * 2 * width
        if zt % 2 == 0:
            return decayed[:, base:base + 8 * SIDE]
        return pltpu.roll(decayed[:, base + width - SIDE:base + 2 * width], 8 * SIDE - SIDE, 1)

    for zt in range(nz):
        for xt in range(0, nx, 2):
            at = zt * nx * 8 + xt * 8
            high, low = halves(jnp.concatenate([span_columns(zt, xt), span_columns(zt, xt + 1)], axis=0))
            lhs[0, at:at + 16, :] = high
            lhs[1, at:at + 16, :] = low
    loads[4].wait()
    tall = owners * 8 // 2
    for group in range(2):
        at = slice(group * tall, (group + 1) * tall)
        coeff = dot(lhs[0, at, :], spread[0]) + dot(lhs[1, at, :], spread[0]) + dot(lhs[0, at, :], spread[1])
        for g in range(tall // 8):
            zt, xt = group * nz // 2 + g // nx, g % nx
            f = xt * nz + zt
            j_own, j_other = selected(f)
            direct = other = jnp.zeros((8, 128), F32)
            for t in range(4):
                piece = coeff[8 * g:8 * g + 8, 128 * t:128 * t + 128]
                direct = jnp.where(j_own // 2 == t, piece, direct)
                other = jnp.where(j_other // 2 == t, piece, other)
            picked = jnp.where((j_own & 1) == half, direct, pltpu.roll(other, 64, 1))
            total = None
            for a in range(8):
                term = weights[8 * a:8 * a + 8, f * 128:f * 128 + 128] * jnp.broadcast_to(picked[a:a + 1, :], (8, 128))
                total = term if total is None else total + term
            part[zt, xt] = total
    pl.semaphore_wait(barrier, nz - 1 + nx * ny - jnp.where(keeps_own, 1, 0) + 1)
    for d in outward(nz)[:-1]:
        zt = lax.rem(z + d, nz)
        pltpu.make_async_remote_copy(
            part.at[zt], arrived.at[nz - d - 1], part_send, part_sem,
            device_id=(replica, x * nz + zt), device_id_type=MESH,
        ).start()

    for load in loads[5:]:
        load.start()

    for f in range(0, owners, 2):
        weights_t[:, f * 128:(f + 2) * 128] = dot(rows[64:, :], one_hot(f))
    loads[5].wait()
    c_own = lax.broadcasted_iota(jnp.int32, (all_cols, 128), 0) - spans * fsdp
    s_own = (lax.broadcasted_iota(jnp.int32, (all_cols, 128), 1) & 63) // 8
    pick = jnp.where(jnp.logical_and(c_own == s_own, s_own < spans), 1.0, 0.0).astype(BF16)
    blk_q[...] = dot(sel[...].reshape(nq * nx * 2, all_cols).astype(F32).astype(BF16), pick).astype(jnp.int32)

    around = sorted(range(ny), key=lambda d: (min(d, ny - d), d))
    tiles = [(d, c, r) for d in around for c in range(2) for r in range(per_core)]
    reach = [[n for n, (d, _, _) in enumerate(tiles) if min(d, ny - d) == g] for g in range(ny // 2 + 1)]
    row_half = half[:1]
    for n, (d, c, r) in enumerate(tiles):
        at = ((2 * lax.rem(y + d, ny) + c) * nx + per_core * core + r) * 2
        pair = jnp.where(row_half == 0, blk_q[pl.ds(at, 1), :], blk_q[pl.ds(at + 1, 1), :])
        numbers[0, n:n + 1, :] = pair
        numbers[1, n:n + 1, :] = pltpu.roll(pair, 64, 1)

    pltpu.make_async_copy(arrived, arrived, part_sem).wait()
    for xt in range(nx):
        total = part[z, xt]
        for d in range(nz - 1):
            total = total + arrived[d, xt]
        full[z, xt] = total

    for d in outward(nz)[:-1]:
        pltpu.make_async_remote_copy(
            full.at[z], full.at[z], full_send, full_sem,
            device_id=(replica, x * nz + lax.rem(z + d, nz)), device_id_type=MESH,
        ).start()

    def send_plane(dx, dy):
        xt = lax.rem(x + dx, nx)
        slot = around.index((ny - dy) % ny) * 2 * per_core + core * per_core + row_to
        pltpu.make_async_remote_copy(
            full.at[z, xt], gathered.at[slot], plane_send, plane_sem.at[min(dy, ny - dy)],
            device_id=(2 * lax.rem(y + dy, ny) + core_to, xt * nz + z), device_id_type=MESH,
        ).start()

    targets = [(dx, dy) for dx in range(nx) for dy in range(ny)]
    for dx, dy in sorted(targets, key=lambda t: -min(t[0], nx - t[0]) - min(t[1], ny - t[1])):
        send = functools.partial(send_plane, dx, dy)
        if dx == dy == 0:
            pl.when(jnp.logical_not(keeps_own))(send)
        else:
            send()

    @pl.when(keeps_own)
    def _():
        gathered[core * per_core + row_to] = full[z, x]

    def await_tiles(first, count, sem):
        ref = gathered.at[pl.ds(first, count)]
        pltpu.make_async_copy(ref, ref, sem).wait()

    def gather_group(g):
        slots = reach[g]
        if g == 0:
            pl.when(keeps_own)(lambda: await_tiles(1, len(slots) - 1, plane_sem.at[0]))
            pl.when(jnp.logical_not(keeps_own))(lambda: await_tiles(0, len(slots), plane_sem.at[0]))
        else:
            await_tiles(slots[0], len(slots), plane_sem.at[g])
        for r in range(per_core):
            mine = [n for n in slots if tiles[n][2] == r]
            values = [gathered[n] for n in mine]
            others = [pltpu.roll(value, 64, 1) for value in values]
            here = [jnp.broadcast_to(numbers[0, n:n + 1, :], (8, 128)) for n in mine]
            there = [jnp.broadcast_to(numbers[1, n:n + 1, :], (8, 128)) for n in mine]
            for t in range(4):
                j_t = 2 * t + half
                i_here = [jnp.where((b & 7) == j_t, b // 8, -1) for b in here]
                i_there = [jnp.where((b & 7) == j_t, b // 8, -1) for b in there]
                for i in range(8):
                    at = (slice(8 * i, 8 * i + 8), slice(128 * t, 128 * t + 128))
                    total = None if g == 0 else sums[r, at[0], at[1]]
                    for value, other, h, o in zip(values, others, i_here, i_there):
                        term = jnp.where(h == i, value, jnp.where(o == i, other, 0.0))
                        total = term if total is None else total + term
                    sums[r, at[0], at[1]] = total

    for g in range(len(reach)):
        gather_group(g)

    loads[6].wait()
    loads[7].wait()
    high, low = halves(jnp.concatenate([sums[r] for r in range(per_core)], axis=0))
    across = dot(high, spread_t[0]) + dot(low, spread_t[0]) + dot(high, spread_t[1])
    high, low = halves(across.T)
    stacked = jnp.concatenate([high, low, high], axis=1)
    lanes = per_core * SIDE
    mine = pl.ds(pl.multiple_of(core * lanes, lanes), lanes)
    pieces = []
    strip = width // 2
    for m in range(2):
        at = slice(m * strip, (m + 1) * strip)
        upd_ref[at, mine] = dot(stacked[at, :], inv[...])
        place = upd_ref.at[at, mine]
        piece = pltpu.make_async_remote_copy(
            place, place, upd_send.at[m], upd_sem.at[m], device_id=(sibling, fsdp), device_id_type=MESH
        )
        piece.start()
        pieces.append(piece)

    pltpu.make_async_copy(full.at[pl.ds(0, nz - 1)], full.at[pl.ds(0, nz - 1)], full_sem).wait()
    for p in range(owners // 2):
        parts = []
        for f in (2 * p, 2 * p + 1):
            j_own, j_other = selected(f)
            total = None
            for u in range(8):
                term = weights_t[8 * u:8 * u + 8, f * 128:f * 128 + 128] * jnp.broadcast_to(
                    full[f % nz, f // nz, u:u + 1, :], (8, 128)
                )
                total = term if total is None else total + term
            other = pltpu.roll(total, 64, 1)
            parts.append(jnp.concatenate([
                jnp.where(j_own == 2 * t + half, total, 0.0) + jnp.where(j_other == 2 * t + half, other, 0.0)
                for t in range(4)
            ], axis=1))
        high, low = halves(jnp.concatenate(parts, axis=0))
        lhs[0, 16 * p:16 * p + 16, :] = high
        lhs[1, 16 * p:16 * p + 16, :] = low
    for m in range(2):
        at = slice(m * tall, (m + 1) * tall)
        space = dot(lhs[0, at, :], spread_t[0]) + dot(lhs[1, at, :], spread_t[0]) + dot(lhs[0, at, :], spread_t[1])
        for g in range(0, tall // 8, 2):
            f = m * (tall // 8) + g
            pair = jnp.concatenate([space[8 * g:8 * g + 8, :width], space[8 * g + 8:8 * g + 16, :width]], axis=1)
            at_cols = slice(f * width, (f + 2) * width)
            res_ref[:, at_cols] = decayed[:, at_cols] - pair

    seven = full.at[pl.ds(0, nz - 1)]
    pltpu.make_async_copy(seven, seven, part_send).wait()
    pltpu.make_async_copy(seven, seven, full_send).wait()
    pl.when(keeps_own)(lambda: await_tiles(1, len(tiles) - 1, plane_send))
    pl.when(jnp.logical_not(keeps_own))(lambda: await_tiles(0, len(tiles), plane_send))
    for piece in pieces:
        piece.wait()


def store_kernel(res_vmem, upd_vmem, res_ref, upd_ref, sems):
    stores = [
        pltpu.make_async_copy(source, target, sems.at[n])
        for n, (source, target) in enumerate(((res_vmem, res_ref), (upd_vmem, upd_ref)))
    ]
    for store in stores:
        store.start()
    for store in stores:
        store.wait()


def local(nx, nz, nq, momentum, gradient, selection):
    rows_dev, all_width = momentum.shape[1:]
    owners = nx * nz
    width = all_width // owners
    spans = width // SIDE
    spread, rows, inverse = tables(spans, nz)
    sel = selection.transpose(0, 1, 3, 2)
    spread_t = spread.transpose(0, 2, 1)
    per_core = nx // 2
    hbm = pl.BlockSpec(memory_space=pltpu.HBM)
    vmem = pl.BlockSpec(memory_space=pltpu.VMEM)
    dma = pltpu.SemaphoreType.DMA
    slab = (rows_dev, all_width)
    operands = (momentum[0], gradient[0], sel, *map(jnp.asarray, (spread, spread_t, rows, inverse)))
    res, upd = pl.pallas_call(
        functools.partial(kernel, nx, nz, nq, spans),
        out_shape=(
            pltpu.VMEM(slab, F32),
            pltpu.VMEM((width, nx * SIDE), F32),
        ),
        in_specs=[hbm] * 7,
        out_specs=(vmem, vmem),
        scratch_shapes=[
            pltpu.VMEM(slab, F32),
            pltpu.VMEM(slab, BF16),
            pltpu.VMEM(sel.shape, jnp.int32),
            pltpu.VMEM(sel.shape[2:], jnp.int32),
            pltpu.VMEM(spread.shape, BF16),
            pltpu.VMEM(spread.shape, BF16),
            pltpu.VMEM(rows.shape[1:], BF16),
            pltpu.VMEM(inverse.shape, BF16),
            pltpu.VMEM(slab, F32),
            pltpu.VMEM((2, owners * 8, 8 * SIDE), BF16),
            pltpu.VMEM((owners, 128), jnp.int32),
            pltpu.VMEM((nq * nx * 2, 128), jnp.int32),
            pltpu.VMEM((2, nq * per_core, 128), jnp.int32),
            pltpu.VMEM((64, owners * 128), F32),
            pltpu.VMEM((64, owners * 128), F32),
            pltpu.VMEM((nz, nx, 8, 128), F32),
            pltpu.VMEM((nz - 1, nx, 8, 128), F32),
            pltpu.VMEM((nz, nx, 8, 128), F32),
            pltpu.VMEM((nq * per_core, 8, 128), F32),
            pltpu.VMEM((per_core, SIDE, 8 * SIDE), F32),
            dma((8,)), dma, dma, dma, dma, dma, dma((nq // 4 + 1,)), dma((2,)), dma((2,)),
        ],
        compiler_params=pltpu.CompilerParams(
            collective_id=0, has_side_effects=True, vmem_limit_bytes=24 * 1024 * 1024
        ),
    )(*(pltpu.with_memory_space_constraint(array, pltpu.HBM) for array in operands))
    res, upd = pl.pallas_call(
        store_kernel,
        out_shape=(jax.ShapeDtypeStruct(slab, F32), jax.ShapeDtypeStruct(upd.shape, F32)),
        in_specs=[vmem] * 2,
        out_specs=(hbm, hbm),
        scratch_shapes=[dma((2,))],
        compiler_params=pltpu.CompilerParams(vmem_limit_bytes=4 * 1024 * 1024),
    )(*(pltpu.with_memory_space_constraint(array, pltpu.VMEM) for array in (res, upd)))
    return res[None], upd.T


def solution(mesh):
    nq = mesh.shape["replica"]
    nz = 8
    nx = mesh.shape["fsdp"] // nz
    return jax.shard_map(
        functools.partial(local, nx, nz, nq),
        mesh=mesh,
        in_specs=(P("replica", "fsdp", None), P("replica", "fsdp", None), P()),
        out_specs=(P("replica", "fsdp", None), P(None, "fsdp")),
        check_vma=False,
    )
```

```python
import functools

import jax
import jax.numpy as jnp
import numpy as np
from jax import lax
from jax.experimental import pallas as pl
from jax.experimental.pallas import tpu as pltpu
from jax.sharding import PartitionSpec as P

SIDE = 64
BLOCK = 8
MESH = pl.DeviceIdType.MESH
F32 = jnp.float32
BF16 = jnp.bfloat16


def cosine_table():
    freq = np.arange(SIDE, dtype=np.float64)[:, None]
    place = np.arange(SIDE, dtype=np.float64)[None, :]
    scale = np.where(freq == 0, np.sqrt(1.0 / SIDE), np.sqrt(2.0 / SIDE))
    return scale * np.cos(np.pi * (2.0 * place + 1.0) * freq / (2.0 * SIDE))


def halves_np(value):
    value = value.astype(np.float32)
    high = value.astype(BF16)
    low = (value - high.astype(np.float32)).astype(BF16)
    return high, low


def tables(spans, devices_z):
    table = cosine_table()
    spread = np.zeros((8 * SIDE, 8, 8, BLOCK))
    for s in range(spans):
        spread[s * SIDE:(s + 1) * SIDE, :, s, :] = table.T.reshape(SIDE, 8, BLOCK)
    spread = np.stack(halves_np(spread.reshape(8 * SIDE, 8 * SIDE)))
    cube = table.reshape(8, BLOCK, devices_z, 8)
    by_a = cube.transpose(2, 3, 1, 0).reshape(devices_z, 64, 8)
    by_u = cube.transpose(2, 1, 3, 0).reshape(devices_z, 64, 8)
    rows = np.concatenate([by_a, by_u], axis=1)
    rows = np.concatenate(halves_np(rows), axis=-1)
    high, low = halves_np(np.kron(np.eye(2), table))
    inverse = np.concatenate([high, high, low], axis=0)
    return spread, rows, inverse


def halves(value):
    high = value.astype(BF16)
    low = (value - high.astype(F32)).astype(BF16)
    return high, low


def dot(a, b):
    return jnp.dot(a, b, preferred_element_type=F32)


def kernel(
    nx, nz, nq, spans,
    mom_hbm, grad_hbm, sel_hbm, spread_hbm, spread_t_hbm, rows_hbm, inv_hbm,
    res_ref, upd_ref,
    mom, grad, sel, sel_own, spread, spread_t, rows, inv, decayed, lhs, blk, blk_q, numbers, weights, weights_t,
    part, arrived, full, gathered, sums,
    load_sem, part_send, part_sem, full_send, full_sem, plane_send, plane_sem, upd_send, upd_sem, ready,
):
    replica = lax.axis_index("replica")
    fsdp = lax.axis_index("fsdp")
    x, z = fsdp // nz, lax.rem(fsdp, nz)
    y, core = replica // 2, lax.rem(replica, 2)
    ny = nq // 2
    sibling = replica + 1 - 2 * core
    per_core = nx // 2
    core_to, row_to = x // per_core, lax.rem(x, per_core)
    keeps_own = core == core_to
    width = spans * SIDE
    owners = nx * nz
    all_cols = owners * spans

    def outward(n):
        return sorted(range(n), key=lambda d: -min(d, n - d))

    barrier = pltpu.get_barrier_semaphore()
    first = replica - core
    for d in outward(nz)[:-1]:
        peer = x * nz + lax.rem(z + d, nz)
        pl.semaphore_signal(barrier, inc=1, device_id=(first, peer), device_id_type=MESH)
    pl.semaphore_signal(barrier, inc=1, device_id=(sibling, fsdp), device_id_type=MESH)
    for dy in outward(ny):
        q = 2 * lax.rem(y + dy, ny) + 1
        for r in range(per_core):
            xs = per_core * core + r
            greet = functools.partial(
                pl.semaphore_signal, barrier, inc=1, device_id=(q, xs * nz + z), device_id_type=MESH
            )
            if dy == 0:
                pl.when(jnp.logical_or(q != replica, xs != x))(greet)
            else:
                greet()

    def tell_sibling():
        pl.semaphore_signal(ready, inc=1, device_id=(sibling, fsdp), device_id_type=MESH)

    loads = [
        pltpu.make_async_copy(source, target, load_sem.at[n])
        for n, (source, target) in enumerate((
            (sel_hbm.at[replica, x], sel_own), (rows_hbm.at[z], rows), (mom_hbm, mom), (grad_hbm, grad),
            (spread_hbm, spread), (sel_hbm, sel), (spread_t_hbm, spread_t), (inv_hbm, inv),
        ))
    ]
    for load in loads[:5]:
        load.start()

    half = lax.broadcasted_iota(jnp.int32, (8, 128), 1) // 64
    sub16 = lax.broadcasted_iota(jnp.int32, (16, 128), 0) & 7

    col = lax.broadcasted_iota(jnp.int32, (owners, all_cols), 1)
    row = lax.broadcasted_iota(jnp.int32, (owners, all_cols), 0) * spans
    inside = jnp.logical_and(col >= row, col < row + spans)
    c_f = lax.broadcasted_iota(jnp.int32, (all_cols, 128), 0).astype(F32)
    c_mod = c_f - spans * jnp.floor((c_f + 0.5) * (1.0 / spans))
    l_i = lax.broadcasted_iota(jnp.int32, (all_cols, 128), 1)
    same_span = c_mod == ((l_i & 63) // 8).astype(F32)
    loads[0].wait()
    placed = None
    for k in range(2):
        left = jnp.where(inside, jnp.broadcast_to(sel_own[k:k + 1, :], (owners, all_cols)), 0).astype(F32)
        right = jnp.where(jnp.logical_and(same_span, l_i // 64 == k), 1.0, 0.0)
        term = dot(left.astype(BF16), right.astype(BF16))
        placed = term if placed is None else placed + term
    blk[...] = placed.astype(jnp.int32)

    def one_hot(f):
        ones = []
        for g in (f, f + 1):
            i_sel = jnp.broadcast_to(blk[g:g + 1, :], (16, 128)) // 8
            ones.append(jnp.where(i_sel == sub16, 1.0, 0.0).astype(BF16))
        return jnp.concatenate(ones, axis=1)

    loads[1].wait()
    for f in range(0, owners, 2):
        weights[:, f * 128:(f + 2) * 128] = dot(rows[:64, :], one_hot(f))

    loads[2].wait()
    loads[3].wait()
    decayed[...] = 0.9 * mom[...] + grad[...].astype(F32)

    def selected(f):
        both = jnp.broadcast_to(blk[f:f + 1, :], (8, 128)) & 7
        return both, pltpu.roll(both, 64, 1)

    def span_columns(zt, xt):
        base = (xt * nz + zt) // 2 * 2 * width
        if zt % 2 == 0:
            return decayed[:, base:base + 8 * SIDE]
        return pltpu.roll(decayed[:, base + width - SIDE:base + 2 * width], 8 * SIDE - SIDE, 1)

    for zt in range(nz):
        for xt in range(0, nx, 2):
            at = zt * nx * 8 + xt * 8
            high, low = halves(jnp.concatenate([span_columns(zt, xt), span_columns(zt, xt + 1)], axis=0))
            lhs[0, at:at + 16, :] = high
            lhs[1, at:at + 16, :] = low
    loads[4].wait()
    tall = owners * 8 // 2
    for group in range(2):
        at = slice(group * tall, (group + 1) * tall)
        coeff = dot(lhs[0, at, :], spread[0]) + dot(lhs[1, at, :], spread[0]) + dot(lhs[0, at, :], spread[1])
        for g in range(tall // 8):
            zt, xt = group * nz // 2 + g // nx, g % nx
            f = xt * nz + zt
            j_own, j_other = selected(f)
            direct = other = jnp.zeros((8, 128), F32)
            for t in range(4):
                piece = coeff[8 * g:8 * g + 8, 128 * t:128 * t + 128]
                direct = jnp.where(j_own // 2 == t, piece, direct)
                other = jnp.where(j_other // 2 == t, piece, other)
            picked = jnp.where((j_own & 1) == half, direct, pltpu.roll(other, 64, 1))
            total = None
            for a in range(8):
                term = weights[8 * a:8 * a + 8, f * 128:f * 128 + 128] * jnp.broadcast_to(picked[a:a + 1, :], (8, 128))
                total = term if total is None else total + term
            part[zt, xt] = total

    @pl.when(core == 0)
    def _():
        pl.semaphore_wait(barrier, 2 * (nz - 1) + 1)
        tell_sibling()

    @pl.when(core == 1)
    def _():
        pl.semaphore_wait(ready, 1)

    for d in outward(nz)[:-1]:
        zt = lax.rem(z + d, nz)
        pltpu.make_async_remote_copy(
            part.at[zt], arrived.at[nz - d - 1], part_send, part_sem,
            device_id=(replica, x * nz + zt), device_id_type=MESH,
        ).start()

    for load in loads[5:]:
        load.start()

    for f in range(0, owners, 2):
        weights_t[:, f * 128:(f + 2) * 128] = dot(rows[64:, :], one_hot(f))
    loads[5].wait()
    c_own = lax.broadcasted_iota(jnp.int32, (all_cols, 128), 0) - spans * fsdp
    s_own = (lax.broadcasted_iota(jnp.int32, (all_cols, 128), 1) & 63) // 8
    pick = jnp.where(jnp.logical_and(c_own == s_own, s_own < spans), 1.0, 0.0).astype(BF16)
    blk_q[...] = dot(sel[...].reshape(nq * nx * 2, all_cols).astype(F32).astype(BF16), pick).astype(jnp.int32)

    around = sorted(range(ny), key=lambda d: (min(d, ny - d), d))
    tiles = [(d, c, r) for d in around for c in range(2) for r in range(per_core)]
    reach = [[n for n, (d, _, _) in enumerate(tiles) if min(d, ny - d) == g] for g in range(ny // 2 + 1)]
    row_half = half[:1]
    for n, (d, c, r) in enumerate(tiles):
        at = ((2 * lax.rem(y + d, ny) + c) * nx + per_core * core + r) * 2
        pair = jnp.where(row_half == 0, blk_q[pl.ds(at, 1), :], blk_q[pl.ds(at + 1, 1), :])
        numbers[0, n:n + 1, :] = pair
        numbers[1, n:n + 1, :] = pltpu.roll(pair, 64, 1)

    @pl.when(core == 1)
    def _():
        pl.semaphore_wait(barrier, nx * ny - jnp.where(keeps_own, 1, 0) + 1)
        tell_sibling()

    pltpu.make_async_copy(arrived, arrived, part_sem).wait()

    @pl.when(core == 0)
    def _():
        pl.semaphore_wait(ready, 1)

    for xt in range(nx):
        total = part[z, xt]
        for d in range(nz - 1):
            total = total + arrived[d, xt]
        full[z, xt] = total

    def send_plane(dx, dy):
        xt = lax.rem(x + dx, nx)
        slot = around.index((ny - dy) % ny) * 2 * per_core + core * per_core + row_to
        pltpu.make_async_remote_copy(
            full.at[z, xt], gathered.at[slot], plane_send, plane_sem.at[min(dy, ny - dy)],
            device_id=(2 * lax.rem(y + dy, ny) + core_to, xt * nz + z), device_id_type=MESH,
        ).start()

    targets = [(dx, dy) for dx in range(nx) for dy in range(ny)]
    for dx, dy in sorted(targets, key=lambda t: -min(t[0], nx - t[0]) - min(t[1], ny - t[1])):
        send = functools.partial(send_plane, dx, dy)
        if dx == dy == 0:
            pl.when(jnp.logical_not(keeps_own))(send)
        else:
            send()

    for d in outward(nz)[:-1]:
        pltpu.make_async_remote_copy(
            full.at[z], full.at[z], full_send, full_sem,
            device_id=(replica, x * nz + lax.rem(z + d, nz)), device_id_type=MESH,
        ).start()

    @pl.when(keeps_own)
    def _():
        gathered[core * per_core + row_to] = full[z, x]

    def await_tiles(first, count, sem):
        ref = gathered.at[pl.ds(first, count)]
        pltpu.make_async_copy(ref, ref, sem).wait()

    def gather_group(g):
        slots = reach[g]
        if g == 0:
            pl.when(keeps_own)(lambda: await_tiles(1, len(slots) - 1, plane_sem.at[0]))
            pl.when(jnp.logical_not(keeps_own))(lambda: await_tiles(0, len(slots), plane_sem.at[0]))
        else:
            await_tiles(slots[0], len(slots), plane_sem.at[g])
        for r in range(per_core):
            mine = [n for n in slots if tiles[n][2] == r]
            values = [gathered[n] for n in mine]
            others = [pltpu.roll(value, 64, 1) for value in values]
            here = [jnp.broadcast_to(numbers[0, n:n + 1, :], (8, 128)) for n in mine]
            there = [jnp.broadcast_to(numbers[1, n:n + 1, :], (8, 128)) for n in mine]
            for t in range(4):
                j_t = 2 * t + half
                i_here = [jnp.where((b & 7) == j_t, b // 8, -1) for b in here]
                i_there = [jnp.where((b & 7) == j_t, b // 8, -1) for b in there]
                for i in range(8):
                    at = (slice(8 * i, 8 * i + 8), slice(128 * t, 128 * t + 128))
                    total = None if g == 0 else sums[r, at[0], at[1]]
                    for value, other, h, o in zip(values, others, i_here, i_there):
                        term = jnp.where(h == i, value, jnp.where(o == i, other, 0.0))
                        total = term if total is None else total + term
                    sums[r, at[0], at[1]] = total

    for g in range(len(reach)):
        gather_group(g)

    loads[6].wait()
    loads[7].wait()
    high, low = halves(jnp.concatenate([sums[r] for r in range(per_core)], axis=0))
    across = dot(high, spread_t[0]) + dot(low, spread_t[0]) + dot(high, spread_t[1])
    high, low = halves(across.T)
    stacked = jnp.concatenate([high, low, high], axis=1)
    lanes = per_core * SIDE
    mine = pl.ds(pl.multiple_of(core * lanes, lanes), lanes)
    pieces = []
    strip = width // 2
    for m in range(2):
        at = slice(m * strip, (m + 1) * strip)
        upd_ref[at, mine] = dot(stacked[at, :], inv[...])
        place = upd_ref.at[at, mine]
        piece = pltpu.make_async_remote_copy(
            place, place, upd_send.at[m], upd_sem.at[m], device_id=(sibling, fsdp), device_id_type=MESH
        )
        piece.start()
        pieces.append(piece)

    pltpu.make_async_copy(full.at[pl.ds(0, nz - 1)], full.at[pl.ds(0, nz - 1)], full_sem).wait()
    for p in range(owners // 2):
        parts = []
        for f in (2 * p, 2 * p + 1):
            j_own, j_other = selected(f)
            total = None
            for u in range(8):
                term = weights_t[8 * u:8 * u + 8, f * 128:f * 128 + 128] * jnp.broadcast_to(
                    full[f % nz, f // nz, u:u + 1, :], (8, 128)
                )
                total = term if total is None else total + term
            other = pltpu.roll(total, 64, 1)
            parts.append(jnp.concatenate([
                jnp.where(j_own == 2 * t + half, total, 0.0) + jnp.where(j_other == 2 * t + half, other, 0.0)
                for t in range(4)
            ], axis=1))
        high, low = halves(jnp.concatenate(parts, axis=0))
        lhs[0, 16 * p:16 * p + 16, :] = high
        lhs[1, 16 * p:16 * p + 16, :] = low
    for m in range(2):
        at = slice(m * tall, (m + 1) * tall)
        space = dot(lhs[0, at, :], spread_t[0]) + dot(lhs[1, at, :], spread_t[0]) + dot(lhs[0, at, :], spread_t[1])
        for g in range(0, tall // 8, 2):
            f = m * (tall // 8) + g
            pair = jnp.concatenate([space[8 * g:8 * g + 8, :width], space[8 * g + 8:8 * g + 16, :width]], axis=1)
            at_cols = slice(f * width, (f + 2) * width)
            res_ref[:, at_cols] = decayed[:, at_cols] - pair

    seven = full.at[pl.ds(0, nz - 1)]
    pltpu.make_async_copy(seven, seven, part_send).wait()
    pltpu.make_async_copy(seven, seven, full_send).wait()
    pl.when(keeps_own)(lambda: await_tiles(1, len(tiles) - 1, plane_send))
    pl.when(jnp.logical_not(keeps_own))(lambda: await_tiles(0, len(tiles), plane_send))
    for piece in pieces:
        piece.wait()


def store_kernel(res_vmem, upd_vmem, res_ref, upd_ref, sems):
    stores = [
        pltpu.make_async_copy(source, target, sems.at[n])
        for n, (source, target) in enumerate(((res_vmem, res_ref), (upd_vmem, upd_ref)))
    ]
    for store in stores:
        store.start()
    for store in stores:
        store.wait()


def local(nx, nz, nq, momentum, gradient, selection):
    rows_dev, all_width = momentum.shape[1:]
    owners = nx * nz
    width = all_width // owners
    spans = width // SIDE
    spread, rows, inverse = tables(spans, nz)
    sel = selection.transpose(0, 1, 3, 2)
    spread_t = spread.transpose(0, 2, 1)
    per_core = nx // 2
    hbm = pl.BlockSpec(memory_space=pltpu.HBM)
    vmem = pl.BlockSpec(memory_space=pltpu.VMEM)
    dma = pltpu.SemaphoreType.DMA
    slab = (rows_dev, all_width)
    operands = (momentum[0], gradient[0], sel, *map(jnp.asarray, (spread, spread_t, rows, inverse)))
    res, upd = pl.pallas_call(
        functools.partial(kernel, nx, nz, nq, spans),
        out_shape=(
            pltpu.VMEM(slab, F32),
            pltpu.VMEM((width, nx * SIDE), F32),
        ),
        in_specs=[hbm] * 7,
        out_specs=(vmem, vmem),
        scratch_shapes=[
            pltpu.VMEM(slab, F32),
            pltpu.VMEM(slab, BF16),
            pltpu.VMEM(sel.shape, jnp.int32),
            pltpu.VMEM(sel.shape[2:], jnp.int32),
            pltpu.VMEM(spread.shape, BF16),
            pltpu.VMEM(spread.shape, BF16),
            pltpu.VMEM(rows.shape[1:], BF16),
            pltpu.VMEM(inverse.shape, BF16),
            pltpu.VMEM(slab, F32),
            pltpu.VMEM((2, owners * 8, 8 * SIDE), BF16),
            pltpu.VMEM((owners, 128), jnp.int32),
            pltpu.VMEM((nq * nx * 2, 128), jnp.int32),
            pltpu.VMEM((2, nq * per_core, 128), jnp.int32),
            pltpu.VMEM((64, owners * 128), F32),
            pltpu.VMEM((64, owners * 128), F32),
            pltpu.VMEM((nz, nx, 8, 128), F32),
            pltpu.VMEM((nz - 1, nx, 8, 128), F32),
            pltpu.VMEM((nz, nx, 8, 128), F32),
            pltpu.VMEM((nq * per_core, 8, 128), F32),
            pltpu.VMEM((per_core, SIDE, 8 * SIDE), F32),
            dma((8,)), dma, dma, dma, dma, dma, dma((nq // 4 + 1,)), dma((2,)), dma((2,)), pltpu.SemaphoreType.REGULAR,
        ],
        compiler_params=pltpu.CompilerParams(
            collective_id=0, has_side_effects=True, vmem_limit_bytes=24 * 1024 * 1024
        ),
    )(*(pltpu.with_memory_space_constraint(array, pltpu.HBM) for array in operands))
    res, upd = pl.pallas_call(
        store_kernel,
        out_shape=(jax.ShapeDtypeStruct(slab, F32), jax.ShapeDtypeStruct(upd.shape, F32)),
        in_specs=[vmem] * 2,
        out_specs=(hbm, hbm),
        scratch_shapes=[dma((2,))],
        compiler_params=pltpu.CompilerParams(vmem_limit_bytes=4 * 1024 * 1024),
    )(*(pltpu.with_memory_space_constraint(array, pltpu.VMEM) for array in (res, upd)))
    return res[None], upd.T


def solution(mesh):
    nq = mesh.shape["replica"]
    nz = 8
    nx = mesh.shape["fsdp"] // nz
    return jax.shard_map(
        functools.partial(local, nx, nz, nq),
        mesh=mesh,
        in_specs=(P("replica", "fsdp", None), P("replica", "fsdp", None), P()),
        out_specs=(P("replica", "fsdp", None), P(None, "fsdp")),
        check_vma=False,
    )
```

```python
import functools

import jax
import jax.numpy as jnp
import numpy as np
from jax import lax
from jax.experimental import pallas as pl
from jax.experimental.pallas import tpu as pltpu
from jax.sharding import PartitionSpec as P

SIDE = 64
BLOCK = 8
MESH = pl.DeviceIdType.MESH
F32 = jnp.float32
BF16 = jnp.bfloat16


def cosine_table():
    freq = np.arange(SIDE, dtype=np.float64)[:, None]
    place = np.arange(SIDE, dtype=np.float64)[None, :]
    scale = np.where(freq == 0, np.sqrt(1.0 / SIDE), np.sqrt(2.0 / SIDE))
    return scale * np.cos(np.pi * (2.0 * place + 1.0) * freq / (2.0 * SIDE))


def halves_np(value):
    value = value.astype(np.float32)
    high = value.astype(BF16)
    low = (value - high.astype(np.float32)).astype(BF16)
    return high, low


def tables(spans, devices_z):
    table = cosine_table()
    spread = np.zeros((8 * SIDE, 8, 8, BLOCK))
    for s in range(spans):
        spread[s * SIDE:(s + 1) * SIDE, :, s, :] = table.T.reshape(SIDE, 8, BLOCK)
    spread = np.stack(halves_np(spread.reshape(8 * SIDE, 8 * SIDE)))
    cube = table.reshape(8, BLOCK, devices_z, 8)
    by_a = cube.transpose(2, 3, 1, 0).reshape(devices_z, 64, 8)
    by_u = cube.transpose(2, 1, 3, 0).reshape(devices_z, 64, 8)
    rows = np.concatenate([by_a, by_u], axis=1)
    rows = np.concatenate(halves_np(rows), axis=-1)
    high, low = halves_np(np.kron(np.eye(2), table))
    inverse = np.concatenate([high, high, low], axis=0)
    return spread, rows, inverse


def halves(value):
    high = value.astype(BF16)
    low = (value - high.astype(F32)).astype(BF16)
    return high, low


def dot(a, b):
    return jnp.dot(a, b, preferred_element_type=F32)


def kernel(
    nx, nz, nq, spans,
    mom_hbm, grad_hbm, sel_hbm, spread_hbm, spread_t_hbm, rows_hbm, inv_hbm,
    res_ref, upd_ref,
    mom, grad, sel, sel_own, spread, spread_t, rows, inv, decayed, lhs, blk, blk_q, numbers, keys, weights, weights_t,
    part, arrived, full, gathered, sums,
    load_sem, part_send, part_sem, full_send, full_sem, plane_send, plane_sem, upd_send, upd_sem, ready,
):
    replica = lax.axis_index("replica")
    fsdp = lax.axis_index("fsdp")
    x, z = fsdp // nz, lax.rem(fsdp, nz)
    y, core = replica // 2, lax.rem(replica, 2)
    ny = nq // 2
    sibling = replica + 1 - 2 * core
    per_core = nx // 2
    core_to, row_to = x // per_core, lax.rem(x, per_core)
    keeps_own = core == core_to
    width = spans * SIDE
    owners = nx * nz
    all_cols = owners * spans

    def outward(n):
        return sorted(range(n), key=lambda d: -min(d, n - d))

    barrier = pltpu.get_barrier_semaphore()
    first = replica - core
    for d in outward(nz)[:-1]:
        peer = x * nz + lax.rem(z + d, nz)
        pl.semaphore_signal(barrier, inc=1, device_id=(first, peer), device_id_type=MESH)
    pl.semaphore_signal(barrier, inc=1, device_id=(sibling, fsdp), device_id_type=MESH)
    loads = [
        pltpu.make_async_copy(source, target, load_sem.at[n])
        for n, (source, target) in enumerate((
            (sel_hbm.at[replica, x], sel_own), (rows_hbm.at[z], rows), (mom_hbm, mom), (grad_hbm, grad),
            (spread_hbm, spread), (sel_hbm, sel), (spread_t_hbm, spread_t), (inv_hbm, inv),
        ))
    ]
    for load in loads[:5]:
        load.start()

    for dy in outward(ny):
        q = 2 * lax.rem(y + dy, ny) + 1
        for r in range(per_core):
            xs = per_core * core + r
            greet = functools.partial(
                pl.semaphore_signal, barrier, inc=1, device_id=(q, xs * nz + z), device_id_type=MESH
            )
            if dy == 0:
                pl.when(jnp.logical_or(q != replica, xs != x))(greet)
            else:
                greet()

    def tell_sibling():
        pl.semaphore_signal(ready, inc=1, device_id=(sibling, fsdp), device_id_type=MESH)

    half = lax.broadcasted_iota(jnp.int32, (8, 128), 1) // 64
    sub16 = lax.broadcasted_iota(jnp.int32, (16, 128), 0) & 7

    col = lax.broadcasted_iota(jnp.int32, (owners, all_cols), 1)
    row = lax.broadcasted_iota(jnp.int32, (owners, all_cols), 0) * spans
    inside = jnp.logical_and(col >= row, col < row + spans)
    c_f = lax.broadcasted_iota(jnp.int32, (all_cols, 128), 0).astype(F32)
    c_mod = c_f - spans * jnp.floor((c_f + 0.5) * (1.0 / spans))
    l_i = lax.broadcasted_iota(jnp.int32, (all_cols, 128), 1)
    same_span = c_mod == ((l_i & 63) // 8).astype(F32)
    loads[0].wait()
    placed = None
    for k in range(2):
        left = jnp.where(inside, jnp.broadcast_to(sel_own[k:k + 1, :], (owners, all_cols)), 0).astype(F32)
        right = jnp.where(jnp.logical_and(same_span, l_i // 64 == k), 1.0, 0.0)
        term = dot(left.astype(BF16), right.astype(BF16))
        placed = term if placed is None else placed + term
    blk[...] = placed.astype(jnp.int32)

    def one_hot(f):
        ones = []
        for g in (f, f + 1):
            i_sel = jnp.broadcast_to(blk[g:g + 1, :], (16, 128)) >> 3
            ones.append(jnp.where(i_sel == sub16, 1.0, 0.0).astype(BF16))
        return jnp.concatenate(ones, axis=1)

    loads[1].wait()
    for f in range(0, owners, 2):
        weights[:, f * 128:(f + 2) * 128] = dot(rows[:64, :], one_hot(f))

    loads[2].wait()
    loads[3].wait()
    decayed[...] = 0.9 * mom[...] + grad[...].astype(F32)

    def selected(f):
        both = jnp.broadcast_to(blk[f:f + 1, :], (8, 128)) & 7
        return both, pltpu.roll(both, 64, 1)

    def span_columns(zt, xt):
        base = (xt * nz + zt) // 2 * 2 * width
        if zt % 2 == 0:
            return decayed[:, base:base + 8 * SIDE]
        return pltpu.roll(decayed[:, base + width - SIDE:base + 2 * width], 8 * SIDE - SIDE, 1)

    for zt in range(nz):
        for xt in range(0, nx, 2):
            at = zt * nx * 8 + xt * 8
            high, low = halves(jnp.concatenate([span_columns(zt, xt), span_columns(zt, xt + 1)], axis=0))
            lhs[0, at:at + 16, :] = high
            lhs[1, at:at + 16, :] = low
    loads[4].wait()
    tall = owners * 8 // 2
    for group in range(2):
        at = slice(group * tall, (group + 1) * tall)
        coeff = dot(lhs[0, at, :], spread[0]) + dot(lhs[1, at, :], spread[0]) + dot(lhs[0, at, :], spread[1])
        for g in range(tall // 8):
            zt, xt = group * nz // 2 + g // nx, g % nx
            f = xt * nz + zt
            j_own, j_other = selected(f)
            direct = other = jnp.zeros((8, 128), F32)
            for t in range(4):
                piece = coeff[8 * g:8 * g + 8, 128 * t:128 * t + 128]
                direct = jnp.where(j_own >> 1 == t, piece, direct)
                other = jnp.where(j_other >> 1 == t, piece, other)
            picked = jnp.where((j_own & 1) == half, direct, pltpu.roll(other, 64, 1))
            total = None
            for a in range(8):
                term = weights[8 * a:8 * a + 8, f * 128:f * 128 + 128] * jnp.broadcast_to(picked[a:a + 1, :], (8, 128))
                total = term if total is None else total + term
            part[zt, xt] = total

    @pl.when(core == 0)
    def _():
        pl.semaphore_wait(barrier, 2 * (nz - 1) + 1)
        tell_sibling()

    @pl.when(core == 1)
    def _():
        pl.semaphore_wait(ready, 1)

    for d in outward(nz)[:-1]:
        zt = lax.rem(z + d, nz)
        pltpu.make_async_remote_copy(
            part.at[zt], arrived.at[nz - d - 1], part_send, part_sem,
            device_id=(replica, x * nz + zt), device_id_type=MESH,
        ).start()

    for load in loads[5:]:
        load.start()

    for f in range(0, owners, 2):
        weights_t[:, f * 128:(f + 2) * 128] = dot(rows[64:, :], one_hot(f))
    loads[5].wait()
    c_own = lax.broadcasted_iota(jnp.int32, (all_cols, 128), 0) - spans * fsdp
    s_own = (lax.broadcasted_iota(jnp.int32, (all_cols, 128), 1) & 63) // 8
    pick = jnp.where(jnp.logical_and(c_own == s_own, s_own < spans), 1.0, 0.0).astype(BF16)
    blk_q[...] = dot(sel[...].reshape(nq * nx * 2, all_cols).astype(F32).astype(BF16), pick).astype(jnp.int32)

    around = sorted(range(ny), key=lambda d: (min(d, ny - d), d))
    tiles = [(d, c, r) for d in around for c in range(2) for r in range(per_core)]
    reach = [[n for n, (d, _, _) in enumerate(tiles) if min(d, ny - d) == g] for g in range(ny // 2 + 1)]
    row_half = half[:1]
    for n, (d, c, r) in enumerate(tiles):
        at = ((2 * lax.rem(y + d, ny) + c) * nx + per_core * core + r) * 2
        pair = jnp.where(row_half == 0, blk_q[pl.ds(at, 1), :], blk_q[pl.ds(at + 1, 1), :])
        numbers[0, n:n + 1, :] = pair
        numbers[1, n:n + 1, :] = pltpu.roll(pair, 64, 1)

    lane_half = lax.broadcasted_iota(jnp.int32, (len(tiles), 128), 1) >> 6
    for side in range(2):
        number = numbers[side]
        for t in range(4):
            keys[side, t] = jnp.where((number & 7) == 2 * t + lane_half, number >> 3, -1)

    @pl.when(core == 1)
    def _():
        pl.semaphore_wait(barrier, nx * ny - jnp.where(keeps_own, 1, 0) + 1)
        tell_sibling()

    pltpu.make_async_copy(arrived, arrived, part_sem).wait()

    @pl.when(core == 0)
    def _():
        pl.semaphore_wait(ready, 1)

    for xt in range(nx):
        total = part[z, xt]
        for d in range(nz - 1):
            total = total + arrived[d, xt]
        full[z, xt] = total

    def send_plane(dx, dy):
        xt = lax.rem(x + dx, nx)
        slot = around.index((ny - dy) % ny) * 2 * per_core + core * per_core + row_to
        pltpu.make_async_remote_copy(
            full.at[z, xt], gathered.at[slot], plane_send, plane_sem.at[min(dy, ny - dy)],
            device_id=(2 * lax.rem(y + dy, ny) + core_to, xt * nz + z), device_id_type=MESH,
        ).start()

    targets = [(dx, dy) for dx in range(nx) for dy in range(ny)]
    for dx, dy in sorted(targets, key=lambda t: -min(t[0], nx - t[0]) - min(t[1], ny - t[1])):
        send = functools.partial(send_plane, dx, dy)
        if dx == dy == 0:
            pl.when(jnp.logical_not(keeps_own))(send)
        else:
            send()

    for d in outward(nz)[:-1]:
        pltpu.make_async_remote_copy(
            full.at[z], full.at[z], full_send, full_sem,
            device_id=(replica, x * nz + lax.rem(z + d, nz)), device_id_type=MESH,
        ).start()

    @pl.when(keeps_own)
    def _():
        gathered[core * per_core + row_to] = full[z, x]

    def await_tiles(first, count, sem):
        ref = gathered.at[pl.ds(first, count)]
        pltpu.make_async_copy(ref, ref, sem).wait()

    def gather_group(g):
        slots = reach[g]
        if g == 0:
            pl.when(keeps_own)(lambda: await_tiles(1, len(slots) - 1, plane_sem.at[0]))
            pl.when(jnp.logical_not(keeps_own))(lambda: await_tiles(0, len(slots), plane_sem.at[0]))
        else:
            await_tiles(slots[0], len(slots), plane_sem.at[g])
        for r in range(per_core):
            mine = [n for n in slots if tiles[n][2] == r]
            values = [gathered[n] for n in mine]
            others = [pltpu.roll(value, 64, 1) for value in values]
            for t in range(4):
                i_here = [jnp.broadcast_to(keys[0, t, n:n + 1, :], (8, 128)) for n in mine]
                i_there = [jnp.broadcast_to(keys[1, t, n:n + 1, :], (8, 128)) for n in mine]
                for i in range(8):
                    at = (slice(8 * i, 8 * i + 8), slice(128 * t, 128 * t + 128))
                    total = None if g == 0 else sums[r, at[0], at[1]]
                    for value, other, h, o in zip(values, others, i_here, i_there):
                        term = jnp.where(h == i, value, jnp.where(o == i, other, 0.0))
                        total = term if total is None else total + term
                    sums[r, at[0], at[1]] = total

    for g in range(len(reach)):
        gather_group(g)

    loads[6].wait()
    loads[7].wait()
    high, low = halves(jnp.concatenate([sums[r] for r in range(per_core)], axis=0))
    across = dot(high, spread_t[0]) + dot(low, spread_t[0]) + dot(high, spread_t[1])
    high, low = halves(across.T)
    stacked = jnp.concatenate([high, low, high], axis=1)
    lanes = per_core * SIDE
    mine = pl.ds(pl.multiple_of(core * lanes, lanes), lanes)
    pieces = []
    strip = width // 2
    for m in range(2):
        at = slice(m * strip, (m + 1) * strip)
        upd_ref[at, mine] = dot(stacked[at, :], inv[...])
        place = upd_ref.at[at, mine]
        piece = pltpu.make_async_remote_copy(
            place, place, upd_send.at[m], upd_sem.at[m], device_id=(sibling, fsdp), device_id_type=MESH
        )
        piece.start()
        pieces.append(piece)

    pltpu.make_async_copy(full.at[pl.ds(0, nz - 1)], full.at[pl.ds(0, nz - 1)], full_sem).wait()
    for p in range(owners // 2):
        parts = []
        for f in (2 * p, 2 * p + 1):
            j_own, j_other = selected(f)
            total = None
            for u in range(8):
                term = weights_t[8 * u:8 * u + 8, f * 128:f * 128 + 128] * jnp.broadcast_to(
                    full[f % nz, f // nz, u:u + 1, :], (8, 128)
                )
                total = term if total is None else total + term
            other = pltpu.roll(total, 64, 1)
            parts.append(jnp.concatenate([
                jnp.where(j_own == 2 * t + half, total, 0.0) + jnp.where(j_other == 2 * t + half, other, 0.0)
                for t in range(4)
            ], axis=1))
        high, low = halves(jnp.concatenate(parts, axis=0))
        lhs[0, 16 * p:16 * p + 16, :] = high
        lhs[1, 16 * p:16 * p + 16, :] = low
    for m in range(2):
        at = slice(m * tall, (m + 1) * tall)
        space = dot(lhs[0, at, :], spread_t[0]) + dot(lhs[1, at, :], spread_t[0]) + dot(lhs[0, at, :], spread_t[1])
        for g in range(0, tall // 8, 2):
            f = m * (tall // 8) + g
            pair = jnp.concatenate([space[8 * g:8 * g + 8, :width], space[8 * g + 8:8 * g + 16, :width]], axis=1)
            at_cols = slice(f * width, (f + 2) * width)
            res_ref[:, at_cols] = decayed[:, at_cols] - pair

    seven = full.at[pl.ds(0, nz - 1)]
    pltpu.make_async_copy(seven, seven, part_send).wait()
    pltpu.make_async_copy(seven, seven, full_send).wait()
    pl.when(keeps_own)(lambda: await_tiles(1, len(tiles) - 1, plane_send))
    pl.when(jnp.logical_not(keeps_own))(lambda: await_tiles(0, len(tiles), plane_send))
    for piece in pieces:
        piece.wait()


def store_kernel(res_vmem, upd_vmem, res_ref, upd_ref, sems):
    stores = [
        pltpu.make_async_copy(source, target, sems.at[n])
        for n, (source, target) in enumerate(((res_vmem, res_ref), (upd_vmem, upd_ref)))
    ]
    for store in stores:
        store.start()
    for store in stores:
        store.wait()


def local(nx, nz, nq, momentum, gradient, selection):
    rows_dev, all_width = momentum.shape[1:]
    owners = nx * nz
    width = all_width // owners
    spans = width // SIDE
    spread, rows, inverse = tables(spans, nz)
    sel = selection.transpose(0, 1, 3, 2)
    spread_t = spread.transpose(0, 2, 1)
    per_core = nx // 2
    hbm = pl.BlockSpec(memory_space=pltpu.HBM)
    vmem = pl.BlockSpec(memory_space=pltpu.VMEM)
    dma = pltpu.SemaphoreType.DMA
    slab = (rows_dev, all_width)
    operands = (momentum[0], gradient[0], sel, *map(jnp.asarray, (spread, spread_t, rows, inverse)))
    res, upd = pl.pallas_call(
        functools.partial(kernel, nx, nz, nq, spans),
        out_shape=(
            pltpu.VMEM(slab, F32),
            pltpu.VMEM((width, nx * SIDE), F32),
        ),
        in_specs=[hbm] * 7,
        out_specs=(vmem, vmem),
        scratch_shapes=[
            pltpu.VMEM(slab, F32),
            pltpu.VMEM(slab, BF16),
            pltpu.VMEM(sel.shape, jnp.int32),
            pltpu.VMEM(sel.shape[2:], jnp.int32),
            pltpu.VMEM(spread.shape, BF16),
            pltpu.VMEM(spread.shape, BF16),
            pltpu.VMEM(rows.shape[1:], BF16),
            pltpu.VMEM(inverse.shape, BF16),
            pltpu.VMEM(slab, F32),
            pltpu.VMEM((2, owners * 8, 8 * SIDE), BF16),
            pltpu.VMEM((owners, 128), jnp.int32),
            pltpu.VMEM((nq * nx * 2, 128), jnp.int32),
            pltpu.VMEM((2, nq * per_core, 128), jnp.int32),
            pltpu.VMEM((2, 4, nq * per_core, 128), jnp.int32),
            pltpu.VMEM((64, owners * 128), F32),
            pltpu.VMEM((64, owners * 128), F32),
            pltpu.VMEM((nz, nx, 8, 128), F32),
            pltpu.VMEM((nz - 1, nx, 8, 128), F32),
            pltpu.VMEM((nz, nx, 8, 128), F32),
            pltpu.VMEM((nq * per_core, 8, 128), F32),
            pltpu.VMEM((per_core, SIDE, 8 * SIDE), F32),
            dma((8,)), dma, dma, dma, dma, dma, dma((nq // 4 + 1,)), dma((2,)), dma((2,)), pltpu.SemaphoreType.REGULAR,
        ],
        compiler_params=pltpu.CompilerParams(
            collective_id=0, has_side_effects=True, vmem_limit_bytes=24 * 1024 * 1024
        ),
    )(*(pltpu.with_memory_space_constraint(array, pltpu.HBM) for array in operands))
    res, upd = pl.pallas_call(
        store_kernel,
        out_shape=(jax.ShapeDtypeStruct(slab, F32), jax.ShapeDtypeStruct(upd.shape, F32)),
        in_specs=[vmem] * 2,
        out_specs=(hbm, hbm),
        scratch_shapes=[dma((2,))],
        compiler_params=pltpu.CompilerParams(vmem_limit_bytes=4 * 1024 * 1024),
    )(*(pltpu.with_memory_space_constraint(array, pltpu.VMEM) for array in (res, upd)))
    return res[None], upd.T


def solution(mesh):
    nq = mesh.shape["replica"]
    nz = 8
    nx = mesh.shape["fsdp"] // nz
    return jax.shard_map(
        functools.partial(local, nx, nz, nq),
        mesh=mesh,
        in_specs=(P("replica", "fsdp", None), P("replica", "fsdp", None), P()),
        out_specs=(P("replica", "fsdp", None), P(None, "fsdp")),
        check_vma=False,
    )
```

```python
import functools

import jax
import jax.numpy as jnp
import numpy as np
from jax import lax
from jax.experimental import pallas as pl
from jax.experimental.pallas import tpu as pltpu
from jax.sharding import PartitionSpec as P

SIDE = 64
BLOCK = 8
MESH = pl.DeviceIdType.MESH
F32 = jnp.float32
BF16 = jnp.bfloat16


def cosine_table():
    freq = np.arange(SIDE, dtype=np.float64)[:, None]
    place = np.arange(SIDE, dtype=np.float64)[None, :]
    scale = np.where(freq == 0, np.sqrt(1.0 / SIDE), np.sqrt(2.0 / SIDE))
    return scale * np.cos(np.pi * (2.0 * place + 1.0) * freq / (2.0 * SIDE))


def halves_np(value):
    value = value.astype(np.float32)
    high = value.astype(BF16)
    low = (value - high.astype(np.float32)).astype(BF16)
    return high, low


def tables(spans, devices_z):
    table = cosine_table()
    spread = np.zeros((8 * SIDE, 8, 8, BLOCK))
    for s in range(spans):
        spread[s * SIDE:(s + 1) * SIDE, :, s, :] = table.T.reshape(SIDE, 8, BLOCK)
    spread = np.stack(halves_np(spread.reshape(8 * SIDE, 8 * SIDE)))
    cube = table.reshape(8, BLOCK, devices_z, 8)
    by_a = cube.transpose(2, 3, 1, 0).reshape(devices_z, 64, 8)
    by_u = cube.transpose(2, 1, 3, 0).reshape(devices_z, 64, 8)
    rows = np.concatenate([by_a, by_u], axis=1)
    rows = np.concatenate(halves_np(rows), axis=-1)
    high, low = halves_np(np.kron(np.eye(2), table))
    inverse = np.concatenate([high, high, low], axis=0)
    return spread, rows, inverse


def halves(value):
    high = value.astype(BF16)
    low = (value - high.astype(F32)).astype(BF16)
    return high, low


def dot(a, b):
    return jnp.dot(a, b, preferred_element_type=F32)


def kernel(
    nx, nz, nq, spans,
    mom_hbm, grad_hbm, sel_hbm, spread_hbm, spread_t_hbm, rows_hbm, inv_hbm,
    res_ref, upd_ref,
    mom, grad, sel, sel_own, spread, spread_t, rows, inv, decayed, lhs, blk, blk_q, numbers, keys, weights, weights_t,
    part, arrived, full, gathered, sums,
    load_sem, part_send, part_sem, full_send, full_sem, plane_send, plane_sem, upd_send, upd_sem, ready,
):
    replica = lax.axis_index("replica")
    fsdp = lax.axis_index("fsdp")
    x, z = fsdp // nz, lax.rem(fsdp, nz)
    y, core = replica // 2, lax.rem(replica, 2)
    ny = nq // 2
    sibling = replica + 1 - 2 * core
    per_core = nx // 2
    core_to, row_to = x // per_core, lax.rem(x, per_core)
    keeps_own = core == core_to
    width = spans * SIDE
    owners = nx * nz
    all_cols = owners * spans

    def outward(n):
        return sorted(range(n), key=lambda d: -min(d, n - d))

    barrier = pltpu.get_barrier_semaphore()
    first = replica - core
    for d in outward(nz)[:-1]:
        peer = x * nz + lax.rem(z + d, nz)
        pl.semaphore_signal(barrier, inc=1, device_id=(first, peer), device_id_type=MESH)
    pl.semaphore_signal(barrier, inc=1, device_id=(sibling, fsdp), device_id_type=MESH)
    loads = [
        pltpu.make_async_copy(source, target, load_sem.at[n])
        for n, (source, target) in enumerate((
            (sel_hbm.at[replica, x], sel_own), (rows_hbm.at[z], rows), (mom_hbm, mom), (grad_hbm, grad),
            (spread_hbm, spread), (sel_hbm, sel), (spread_t_hbm, spread_t), (inv_hbm, inv),
        ))
    ]
    for load in loads[:5]:
        load.start()

    for dy in outward(ny):
        q = 2 * lax.rem(y + dy, ny) + 1
        for r in range(per_core):
            xs = per_core * core + r
            greet = functools.partial(
                pl.semaphore_signal, barrier, inc=1, device_id=(q, xs * nz + z), device_id_type=MESH
            )
            if dy == 0:
                pl.when(jnp.logical_or(q != replica, xs != x))(greet)
            else:
                greet()

    def tell_sibling():
        pl.semaphore_signal(ready, inc=1, device_id=(sibling, fsdp), device_id_type=MESH)

    half = lax.broadcasted_iota(jnp.int32, (8, 128), 1) // 64
    sub16 = lax.broadcasted_iota(jnp.int32, (16, 128), 0) & 7

    col = lax.broadcasted_iota(jnp.int32, (owners, all_cols), 1)
    row = lax.broadcasted_iota(jnp.int32, (owners, all_cols), 0) * spans
    inside = jnp.logical_and(col >= row, col < row + spans)
    c_f = lax.broadcasted_iota(jnp.int32, (all_cols, 128), 0).astype(F32)
    c_mod = c_f - spans * jnp.floor((c_f + 0.5) * (1.0 / spans))
    l_i = lax.broadcasted_iota(jnp.int32, (all_cols, 128), 1)
    same_span = c_mod == ((l_i & 63) // 8).astype(F32)
    loads[0].wait()
    placed = None
    for k in range(2):
        left = jnp.where(inside, jnp.broadcast_to(sel_own[k:k + 1, :], (owners, all_cols)), 0).astype(F32)
        right = jnp.where(jnp.logical_and(same_span, l_i // 64 == k), 1.0, 0.0)
        term = dot(left.astype(BF16), right.astype(BF16))
        placed = term if placed is None else placed + term
    blk[...] = placed.astype(jnp.int32)

    def one_hot(f):
        ones = []
        for g in (f, f + 1):
            i_sel = jnp.broadcast_to(blk[g:g + 1, :], (16, 128)) >> 3
            ones.append(jnp.where(i_sel == sub16, 1.0, 0.0).astype(BF16))
        return jnp.concatenate(ones, axis=1)

    loads[1].wait()
    for f in range(0, owners, 2):
        weights[:, f * 128:(f + 2) * 128] = dot(rows[:64, :], one_hot(f))

    loads[2].wait()
    loads[3].wait()
    decayed[...] = 0.9 * mom[...] + grad[...].astype(F32)

    def selected(f):
        both = jnp.broadcast_to(blk[f:f + 1, :], (8, 128)) & 7
        return both, pltpu.roll(both, 64, 1)

    def span_columns(zt, xt):
        base = (xt * nz + zt) // 2 * 2 * width
        if zt % 2 == 0:
            return decayed[:, base:base + 8 * SIDE]
        return pltpu.roll(decayed[:, base + width - SIDE:base + 2 * width], 8 * SIDE - SIDE, 1)

    for zt in range(nz):
        for xt in range(0, nx, 2):
            at = zt * nx * 8 + xt * 8
            high, low = halves(jnp.concatenate([span_columns(zt, xt), span_columns(zt, xt + 1)], axis=0))
            lhs[0, at:at + 16, :] = high
            lhs[1, at:at + 16, :] = low
    loads[4].wait()
    tall = owners * 8 // 2
    for group in range(2):
        at = slice(group * tall, (group + 1) * tall)
        coeff = dot(lhs[0, at, :], spread[0]) + dot(lhs[1, at, :], spread[0]) + dot(lhs[0, at, :], spread[1])
        for g in range(tall // 8):
            zt, xt = group * nz // 2 + g // nx, g % nx
            f = xt * nz + zt
            j_own, j_other = selected(f)
            direct = other = jnp.zeros((8, 128), F32)
            for t in range(4):
                piece = coeff[8 * g:8 * g + 8, 128 * t:128 * t + 128]
                direct = jnp.where(j_own >> 1 == t, piece, direct)
                other = jnp.where(j_other >> 1 == t, piece, other)
            picked = jnp.where((j_own & 1) == half, direct, pltpu.roll(other, 64, 1))
            total = None
            for a in range(8):
                term = weights[8 * a:8 * a + 8, f * 128:f * 128 + 128] * jnp.broadcast_to(picked[a:a + 1, :], (8, 128))
                total = term if total is None else total + term
            part[zt, xt] = total

    @pl.when(core == 0)
    def _():
        pl.semaphore_wait(barrier, 2 * (nz - 1) + 1)
        tell_sibling()

    @pl.when(core == 1)
    def _():
        pl.semaphore_wait(ready, 1)

    for d in outward(nz)[:-1]:
        zt = lax.rem(z + d, nz)
        pltpu.make_async_remote_copy(
            part.at[zt], arrived.at[nz - d - 1], part_send, part_sem,
            device_id=(replica, x * nz + zt), device_id_type=MESH,
        ).start()

    for load in loads[5:]:
        load.start()

    for f in range(0, owners, 2):
        weights_t[:, f * 128:(f + 2) * 128] = dot(rows[64:, :], one_hot(f))
    loads[5].wait()
    c_own = lax.broadcasted_iota(jnp.int32, (all_cols, 128), 0) - spans * fsdp
    s_own = (lax.broadcasted_iota(jnp.int32, (all_cols, 128), 1) & 63) // 8
    pick = jnp.where(jnp.logical_and(c_own == s_own, s_own < spans), 1.0, 0.0).astype(BF16)
    blk_q[...] = dot(sel[...].reshape(nq * nx * 2, all_cols).astype(F32).astype(BF16), pick).astype(jnp.int32)

    around = sorted(range(ny), key=lambda d: (min(d, ny - d), d))
    tiles = [(d, c, r) for d in around for c in range(2) for r in range(per_core)]
    reach = [[n for n, (d, _, _) in enumerate(tiles) if min(d, ny - d) == g] for g in range(ny // 2 + 1)]
    row_half = half[:1]
    for n, (d, c, r) in enumerate(tiles):
        at = ((2 * lax.rem(y + d, ny) + c) * nx + per_core * core + r) * 2
        pair = jnp.where(row_half == 0, blk_q[pl.ds(at, 1), :], blk_q[pl.ds(at + 1, 1), :])
        numbers[0, n:n + 1, :] = pair
        numbers[1, n:n + 1, :] = pltpu.roll(pair, 64, 1)

    lane_half = lax.broadcasted_iota(jnp.int32, (len(tiles), 128), 1) >> 6
    for side in range(2):
        number = numbers[side]
        for t in range(4):
            keys[side, t] = jnp.where((number & 7) == 2 * t + lane_half, number >> 3, -1)

    @pl.when(core == 1)
    def _():
        pl.semaphore_wait(barrier, nx * ny - jnp.where(keeps_own, 1, 0) + 1)
        tell_sibling()

    pltpu.make_async_copy(arrived, arrived, part_sem).wait()

    @pl.when(core == 0)
    def _():
        pl.semaphore_wait(ready, 1)

    for xt in range(nx):
        total = part[z, xt]
        for d in range(nz - 1):
            total = total + arrived[d, xt]
        full[z, xt] = total

    def send_plane(dx, dy):
        xt = lax.rem(x + dx, nx)
        slot = around.index((ny - dy) % ny) * 2 * per_core + core * per_core + row_to
        pltpu.make_async_remote_copy(
            full.at[z, xt], gathered.at[slot], plane_send, plane_sem.at[min(dy, ny - dy)],
            device_id=(2 * lax.rem(y + dy, ny) + core_to, xt * nz + z), device_id_type=MESH,
        ).start()

    targets = [(dx, dy) for dx in range(nx) for dy in range(ny)]
    for dx, dy in sorted(targets, key=lambda t: -min(t[0], nx - t[0]) - min(t[1], ny - t[1])):
        send = functools.partial(send_plane, dx, dy)
        if dx == dy == 0:
            pl.when(jnp.logical_not(keeps_own))(send)
        else:
            send()

    for d in outward(nz)[:-1]:
        pltpu.make_async_remote_copy(
            full.at[z], full.at[z], full_send, full_sem,
            device_id=(replica, x * nz + lax.rem(z + d, nz)), device_id_type=MESH,
        ).start()

    @pl.when(keeps_own)
    def _():
        gathered[core * per_core + row_to] = full[z, x]

    def await_tiles(first, count, sem):
        ref = gathered.at[pl.ds(first, count)]
        pltpu.make_async_copy(ref, ref, sem).wait()

    def gather_group(g):
        slots = reach[g]
        if g == 0:
            pl.when(keeps_own)(lambda: await_tiles(1, len(slots) - 1, plane_sem.at[0]))
            pl.when(jnp.logical_not(keeps_own))(lambda: await_tiles(0, len(slots), plane_sem.at[0]))
        else:
            await_tiles(slots[0], len(slots), plane_sem.at[g])
        for r in range(per_core):
            mine = [n for n in slots if tiles[n][2] == r]
            values = [gathered[n] for n in mine]
            others = [pltpu.roll(value, 64, 1) for value in values]
            for t in range(4):
                i_here = [jnp.broadcast_to(keys[0, t, n:n + 1, :], (8, 128)) for n in mine]
                i_there = [jnp.broadcast_to(keys[1, t, n:n + 1, :], (8, 128)) for n in mine]
                for i in range(8):
                    at = (slice(8 * i, 8 * i + 8), slice(128 * t, 128 * t + 128))
                    total = None if g == 0 else sums[r, at[0], at[1]]
                    for value, other, h, o in zip(values, others, i_here, i_there):
                        term = jnp.where(h == i, value, jnp.where(o == i, other, 0.0))
                        total = term if total is None else total + term
                    sums[r, at[0], at[1]] = total

    for g in range(len(reach)):
        gather_group(g)

    loads[6].wait()
    loads[7].wait()
    high, low = halves(jnp.concatenate([sums[r] for r in range(per_core)], axis=0))
    across = dot(high, spread_t[0]) + dot(low, spread_t[0]) + dot(high, spread_t[1])
    high, low = halves(across.T)
    stacked = jnp.concatenate([high, low, high], axis=1)
    lanes = per_core * SIDE
    mine = pl.ds(pl.multiple_of(core * lanes, lanes), lanes)
    pieces = []
    strip = width
    for m in range(1):
        at = slice(m * strip, (m + 1) * strip)
        upd_ref[at, mine] = dot(stacked[at, :], inv[...])
        place = upd_ref.at[at, mine]
        piece = pltpu.make_async_remote_copy(
            place, place, upd_send.at[m], upd_sem.at[m], device_id=(sibling, fsdp), device_id_type=MESH
        )
        piece.start()
        pieces.append(piece)

    pltpu.make_async_copy(full.at[pl.ds(0, nz - 1)], full.at[pl.ds(0, nz - 1)], full_sem).wait()
    for p in range(owners // 2):
        parts = []
        for f in (2 * p, 2 * p + 1):
            j_own, j_other = selected(f)
            total = None
            for u in range(8):
                term = weights_t[8 * u:8 * u + 8, f * 128:f * 128 + 128] * jnp.broadcast_to(
                    full[f % nz, f // nz, u:u + 1, :], (8, 128)
                )
                total = term if total is None else total + term
            other = pltpu.roll(total, 64, 1)
            parts.append(jnp.concatenate([
                jnp.where(j_own == 2 * t + half, total, 0.0) + jnp.where(j_other == 2 * t + half, other, 0.0)
                for t in range(4)
            ], axis=1))
        high, low = halves(jnp.concatenate(parts, axis=0))
        lhs[0, 16 * p:16 * p + 16, :] = high
        lhs[1, 16 * p:16 * p + 16, :] = low
    for m in range(2):
        at = slice(m * tall, (m + 1) * tall)
        space = dot(lhs[0, at, :], spread_t[0]) + dot(lhs[1, at, :], spread_t[0]) + dot(lhs[0, at, :], spread_t[1])
        for g in range(0, tall // 8, 2):
            f = m * (tall // 8) + g
            pair = jnp.concatenate([space[8 * g:8 * g + 8, :width], space[8 * g + 8:8 * g + 16, :width]], axis=1)
            at_cols = slice(f * width, (f + 2) * width)
            res_ref[:, at_cols] = decayed[:, at_cols] - pair

    seven = full.at[pl.ds(0, nz - 1)]
    pltpu.make_async_copy(seven, seven, part_send).wait()
    pltpu.make_async_copy(seven, seven, full_send).wait()
    pl.when(keeps_own)(lambda: await_tiles(1, len(tiles) - 1, plane_send))
    pl.when(jnp.logical_not(keeps_own))(lambda: await_tiles(0, len(tiles), plane_send))
    for piece in pieces:
        piece.wait()


def store_kernel(res_vmem, upd_vmem, res_ref, upd_ref, sems):
    stores = [
        pltpu.make_async_copy(source, target, sems.at[n])
        for n, (source, target) in enumerate(((res_vmem, res_ref), (upd_vmem, upd_ref)))
    ]
    for store in stores:
        store.start()
    for store in stores:
        store.wait()


def local(nx, nz, nq, momentum, gradient, selection):
    rows_dev, all_width = momentum.shape[1:]
    owners = nx * nz
    width = all_width // owners
    spans = width // SIDE
    spread, rows, inverse = tables(spans, nz)
    sel = selection.transpose(0, 1, 3, 2)
    spread_t = spread.transpose(0, 2, 1)
    per_core = nx // 2
    hbm = pl.BlockSpec(memory_space=pltpu.HBM)
    vmem = pl.BlockSpec(memory_space=pltpu.VMEM)
    dma = pltpu.SemaphoreType.DMA
    slab = (rows_dev, all_width)
    operands = (momentum[0], gradient[0], sel, *map(jnp.asarray, (spread, spread_t, rows, inverse)))
    res, upd = pl.pallas_call(
        functools.partial(kernel, nx, nz, nq, spans),
        out_shape=(
            pltpu.VMEM(slab, F32),
            pltpu.VMEM((width, nx * SIDE), F32),
        ),
        in_specs=[hbm] * 7,
        out_specs=(vmem, vmem),
        scratch_shapes=[
            pltpu.VMEM(slab, F32),
            pltpu.VMEM(slab, BF16),
            pltpu.VMEM(sel.shape, jnp.int32),
            pltpu.VMEM(sel.shape[2:], jnp.int32),
            pltpu.VMEM(spread.shape, BF16),
            pltpu.VMEM(spread.shape, BF16),
            pltpu.VMEM(rows.shape[1:], BF16),
            pltpu.VMEM(inverse.shape, BF16),
            pltpu.VMEM(slab, F32),
            pltpu.VMEM((2, owners * 8, 8 * SIDE), BF16),
            pltpu.VMEM((owners, 128), jnp.int32),
            pltpu.VMEM((nq * nx * 2, 128), jnp.int32),
            pltpu.VMEM((2, nq * per_core, 128), jnp.int32),
            pltpu.VMEM((2, 4, nq * per_core, 128), jnp.int32),
            pltpu.VMEM((64, owners * 128), F32),
            pltpu.VMEM((64, owners * 128), F32),
            pltpu.VMEM((nz, nx, 8, 128), F32),
            pltpu.VMEM((nz - 1, nx, 8, 128), F32),
            pltpu.VMEM((nz, nx, 8, 128), F32),
            pltpu.VMEM((nq * per_core, 8, 128), F32),
            pltpu.VMEM((per_core, SIDE, 8 * SIDE), F32),
            dma((8,)), dma, dma, dma, dma, dma, dma((nq // 4 + 1,)), dma((1,)), dma((1,)), pltpu.SemaphoreType.REGULAR,
        ],
        compiler_params=pltpu.CompilerParams(
            collective_id=0, has_side_effects=True, vmem_limit_bytes=24 * 1024 * 1024
        ),
    )(*(pltpu.with_memory_space_constraint(array, pltpu.HBM) for array in operands))
    res, upd = pl.pallas_call(
        store_kernel,
        out_shape=(jax.ShapeDtypeStruct(slab, F32), jax.ShapeDtypeStruct(upd.shape, F32)),
        in_specs=[vmem] * 2,
        out_specs=(hbm, hbm),
        scratch_shapes=[dma((2,))],
        compiler_params=pltpu.CompilerParams(vmem_limit_bytes=4 * 1024 * 1024),
    )(*(pltpu.with_memory_space_constraint(array, pltpu.VMEM) for array in (res, upd)))
    return res[None], upd.T


def solution(mesh):
    nq = mesh.shape["replica"]
    nz = 8
    nx = mesh.shape["fsdp"] // nz
    return jax.shard_map(
        functools.partial(local, nx, nz, nq),
        mesh=mesh,
        in_specs=(P("replica", "fsdp", None), P("replica", "fsdp", None), P()),
        out_specs=(P("replica", "fsdp", None), P(None, "fsdp")),
        check_vma=False,
    )
```
